32 devices in a mesh: group: 2 (over y), shot: 4 (over z), line: 2 (over x), tm: 2 (over core).
Axes of the slice: x: 2, y: 2, z: 4, core: 2. Of those that a mesh axis runs over, the one named last changes fastest.
Arguments:
- initial_guess: bfloat16 [8, 256, 1024], P(('group', 'shot'), 'line', 'tm'), parts along dimension 0
- measured_mixtures: bfloat16 [4, 256, 1024], P('group', 'line'), parts along dimension 0
- launch_lags: int32 [8], P('group'), parts along dimension 0, may hold values from 0 to 127, as said below
- source_launch_order: int32 [8], P('group'), parts along dimension 0, may hold values from 0 to 3, each once
- station_portion_tallies: int32 [16], P('group'), parts along dimension 0, may hold values from 1 to 32, 128 in all
- source_entry_kernel: bfloat16 [4, 3, 64], replicated, may hold values from -1.75 to 1.75
- source_spaced_kernel: bfloat16 [3, 64, 64], replicated, may hold values from -0.4375 to 0.4375
- source_exit_kernel: bfloat16 [4, 64], replicated, may hold values from -0.5 to 0.5
- source_inner_offsets: float32 [2, 64], replicated, may hold values from -3 to 3
- station_entry_kernel: bfloat16 [4, 3, 64], replicated, may hold values from -1.75 to 1.75
- station_spaced_kernel: bfloat16 [3, 64, 64], replicated, may hold values from -0.4375 to 0.4375
- station_exit_kernel: bfloat16 [4, 64], replicated, may hold values from -0.5 to 0.5
- station_inner_offsets: float32 [2, 64], replicated, may hold values from -3 to 3
- learned_pace_factors: float32 [2], replicated, may hold values from 0.3 to 0.8
Outputs:
- deblended: bfloat16 [8, 256, 1024], P(('group', 'shot'), 'line', 'tm'), parts along dimension 0
The draws below stay inside these ranges and needn't reach their ends.
There are 2 independent parts, one for each index of `group`. The reference program is written for one: setup_inputs(seed, part) draws one part's arguments, and reference() takes and returns one part's arrays. A program takes and returns all parts, laid end to end along the dimension named above; an argument that names none is the same for every part. Nothing has to cross between parts.
Inputs may be any that keep to these rules, and one draw needn't show every extreme that they name: `launch_lags`: 0 and 127 both occur. `source_launch_order`: each shot once. `station_portion_tallies`: the counts sum to 128 and the largest equals 32.
All inputs are finite; a program needn't handle non-finite values.
Results may differ from the reference program's by a relative error of at most 0.013.
Values may be sent and summed in bfloat16 or wider, within the bound.
A program may use at most 64 MiB of HBM per device.

```python
import math
import jax
import jax.numpy as jnp
import numpy as np
from jax import lax

LINES = 16
RPL = 16
NT = 1024
FEAT = 64
DMAX = 128
ITERS = 2
TILE_SOURCES = 4
NG = 2
RB = 128
NP = 8
RCAP = 32
N_LINE = 2


def receiver_scales(key):
    sub_key = jax.random.fold_in(key, 11)
    return jnp.exp(jax.random.uniform(sub_key, (LINES * RPL,), jnp.float32, math.log(0.3), math.log(3.0)))


def time_decay():
    fraction = jnp.arange(NT, dtype=jnp.float32) / NT
    return jnp.exp(-math.log(3.0) * fraction)


def draw_initial_guess(key, part):
    rscale = receiver_scales(key)
    shape_full = (TILE_SOURCES, LINES * RPL, NT)
    sscale = jnp.exp(jax.random.uniform(jax.random.fold_in(key, 12), (TILE_SOURCES,), jnp.float32, math.log(0.5), math.log(2.0)))
    noise = jax.random.normal(jax.random.fold_in(key, 13), shape_full, jnp.float32)
    values = noise * sscale[:, None, None] * rscale[None, :, None] * time_decay()[None, None, :]
    return values.astype(jnp.bfloat16)


def draw_measured_mixtures(key, part):
    rscale = receiver_scales(key)
    shape_full = (NG, LINES * RPL, NT)
    noise = 1.4 * jax.random.normal(jax.random.fold_in(key, 15), shape_full, jnp.float32)
    values = noise * rscale[None, :, None] * time_decay()[None, None, :]
    return values.astype(jnp.bfloat16)


def draw_launch_lags(key, part):
    base = jax.random.randint(jax.random.fold_in(key, 21), (TILE_SOURCES,), 0, DMAX)
    lowest = jax.random.randint(jax.random.fold_in(key, 22), (), 0, TILE_SOURCES)
    highest = (lowest + 1 + jax.random.randint(jax.random.fold_in(key, 23), (), 0, TILE_SOURCES - 1)) % TILE_SOURCES
    return base.at[lowest].set(0).at[highest].set(DMAX - 1).astype(jnp.int32)


def split_up(amount, total, bound, skew):
    weights = [(1 << 20) // math.isqrt(grade ** skew) + 1 for grade in range(2, amount + 1)]
    spare, given = total - bound - (amount - 1), [1] * (amount - 1)
    while spare > 0:
        free = [i for i in range(amount - 1) if given[i] < bound]
        pool, budget = sum([weights[i] for i in free]), spare
        for i in free:
            more = min(bound - given[i], max(1, budget * weights[i] // pool), spare)
            given[i] = given[i] + more
            spare = spare - more
    return np.array([bound] + given)


def ragged(own_key, number_of, total, limit, lean):
    if number_of == 2:
        one = jax.random.randint(own_key, (), max(1, total - limit), min(limit, total - 1) + 1)
        return jnp.stack([one, total - one])
    sizes = jnp.asarray(split_up(number_of, total, limit, lean), jnp.int32)
    pairs = (number_of - 1) // 2
    giver, sink = sizes[1:1 + 2 * pairs:2], sizes[2:2 + 2 * pairs:2]
    room = jnp.minimum(giver - 1, limit - sink)
    shifted = jax.random.randint(jax.random.fold_in(own_key, 1), (pairs,), 0, 1 << 20) % (room + 1)
    sizes = sizes.at[1:1 + 2 * pairs:2].set(giver - shifted).at[2:2 + 2 * pairs:2].set(sink + shifted)
    return sizes[jax.random.permutation(jax.random.fold_in(own_key, 2), number_of)]


def centred(key, extent, deviation, limit, kind=jnp.bfloat16):
    entries = jax.random.normal(key, extent, jnp.float32) * deviation
    return jnp.minimum(jnp.maximum(entries, -limit), limit).astype(kind)


def setup_inputs(seed: int = 0, part: int = 0) -> dict:
    splits = jax.random.split(jax.random.key(seed), 15)
    part_splits = jax.random.split(jax.random.fold_in(splits[14], part), 15)
    return {
        "initial_guess": draw_initial_guess(jax.random.fold_in(jax.random.fold_in(splits[14], part), 71), part),
        "measured_mixtures": draw_measured_mixtures(jax.random.fold_in(jax.random.fold_in(splits[14], part), 71), part),
        "launch_lags": draw_launch_lags(jax.random.fold_in(jax.random.fold_in(splits[14], part), 71), part),
        "source_launch_order": jax.random.permutation(part_splits[3], TILE_SOURCES).astype(jnp.int32),
        "station_portion_tallies": ragged(part_splits[4], NP, RB, RCAP, 2).astype(jnp.int32),
        "source_entry_kernel": centred(splits[5], (4, 3, FEAT), 12 ** -0.5, 1.75),
        "source_spaced_kernel": centred(splits[6], (3, FEAT, FEAT), (3 * FEAT) ** -0.5, 0.4375),
        "source_exit_kernel": centred(splits[7], (4, FEAT), (2 * FEAT) ** -0.5, 0.5),
        "source_inner_offsets": centred(splits[8], (2, FEAT), 0.5, 3.0, jnp.float32),
        "station_entry_kernel": centred(splits[9], (4, 3, FEAT), 12 ** -0.5, 1.75),
        "station_spaced_kernel": centred(splits[10], (3, FEAT, FEAT), (3 * FEAT) ** -0.5, 0.4375),
        "station_exit_kernel": centred(splits[11], (4, FEAT), (2 * FEAT) ** -0.5, 0.5),
        "station_inner_offsets": centred(splits[12], (2, FEAT), 0.5, 3.0, jnp.float32),
        "learned_pace_factors": jnp.clip(jnp.exp(jax.random.uniform(splits[13], (ITERS,), jnp.float32, math.log(0.3), math.log(0.8))), 0.3, 0.8),
    }


MARGIN = 7
EPSILON = 1e-05

def network(padded, first_sample, full_len, weight_in, weight_mid, weight_out, bias_pair):
    batch = padded.shape[0]
    sample_extent = padded.shape[2] - 2 * MARGIN
    half_len = sample_extent // 2
    count_one = half_len + 6
    count_two = half_len + 2
    wide_in = padded.astype(jnp.float32)
    total_sum = jnp.zeros((batch, weight_in.shape[2], count_one), jnp.float32)
    for tap_index in range(4):
        tap_slice = wide_in[:, :, tap_index:tap_index + 2 * count_one - 1:2]
        total_sum = total_sum + jnp.einsum('bcv,cf->bfv', tap_slice, weight_in[tap_index].astype(jnp.float32), precision=lax.Precision.HIGHEST)
    where_one = first_sample // 2 - 3 + jnp.arange(count_one)
    keep_one = (where_one >= 0) & (where_one < full_len // 2)
    layer_one = jnp.where(keep_one, jax.nn.relu(total_sum + bias_pair[0][None, :, None]), 0.0).astype(jnp.bfloat16)
    wide_one = layer_one.astype(jnp.float32)
    total_two = jnp.zeros((batch, weight_mid.shape[2], count_two), jnp.float32)
    for tap_index in range(3):
        total_two = total_two + jnp.einsum('bgw,gf->bfw', wide_one[:, :, 2 * tap_index:2 * tap_index + count_two], weight_mid[tap_index].astype(jnp.float32), precision=lax.Precision.HIGHEST)
    where_two = first_sample // 2 - 1 + jnp.arange(count_two)
    keep_two = (where_two >= 0) & (where_two < full_len // 2)
    layer_two = jnp.where(keep_two, jax.nn.relu(total_two + bias_pair[1][None, :, None]), 0.0).astype(jnp.bfloat16)
    projected = jnp.einsum('bgw,kg->bkw', layer_two.astype(jnp.float32), weight_out.astype(jnp.float32), precision=lax.Precision.HIGHEST)
    even_part = projected[:, 1, 1:half_len + 1] + projected[:, 3, 0:half_len]
    odd_part = projected[:, 0, 2:half_len + 2] + projected[:, 2, 1:half_len + 1]
    return jnp.stack([even_part, odd_part], axis=2).reshape(batch, sample_extent)

def sections(station_portion_tallies, block_size):
    offsets = jnp.cumsum(station_portion_tallies) - station_portion_tallies
    places = jnp.arange(block_size, dtype=jnp.int32)
    owner_of = lax.optimization_barrier(jnp.sum((offsets[None, :] <= places[:, None]).astype(jnp.int32), axis=1)) - 1
    return (offsets, owner_of)

def receiver_pass(sorting_choice, rms_scale, weights):
    normed = (sorting_choice.astype(jnp.float32) / rms_scale[:, None, None]).astype(jnp.bfloat16)

    def one_receiver(trace_set):
        shot_count = trace_set.shape[0]
        edged_set = jnp.pad(trace_set, ((1, 1), (0, 0)))
        stacked = jnp.stack([edged_set[channel:channel + shot_count] for channel in range(3)], axis=1)
        inputs = jnp.pad(stacked, ((0, 0), (0, 0), (MARGIN, MARGIN)))
        return network(inputs, 0, trace_set.shape[1], *weights)
    shaped = lax.map(one_receiver, normed)
    return (sorting_choice.astype(jnp.float32) + rms_scale[:, None, None] * shaped).astype(jnp.bfloat16)

def mixture_leftover(sorting_choice, measured_mixtures_here, source_launch_order, launch_lags, correction_pace):
    channel_total, shot_count, sample_extent = sorting_choice.shape
    mixture_batches = measured_mixtures_here.shape[1]
    sources_within_mixture = shot_count // mixture_batches
    widened = jnp.pad(sorting_choice.astype(jnp.float32), ((0, 0), (0, 0), (DMAX, 0)))

    def fire_shot(column, delay_at):
        return lax.dynamic_slice_in_dim(column, (DMAX - delay_at).astype(jnp.int32), sample_extent, axis=1)
    launched_source_collection = jax.vmap(fire_shot, in_axes=(1, 0), out_axes=1)(widened, launch_lags)
    recording_mismatch = jnp.take(launched_source_collection, source_launch_order, axis=1).reshape(channel_total, mixture_batches, sources_within_mixture, sample_extent).sum(axis=2) - measured_mixtures_here.astype(jnp.float32)
    place_labels = jnp.arange(shot_count, dtype=jnp.int32)
    source_location = lax.optimization_barrier(jnp.sum(jnp.where(source_launch_order[None, :] == place_labels[:, None], place_labels[None, :], 0), axis=1)).astype(jnp.int32)
    group_of = source_location // sources_within_mixture
    late_pad = jnp.pad(recording_mismatch, ((0, 0), (0, 0), (0, DMAX)))

    def spread(group_at, delay_at):
        group_row = jnp.take(late_pad, group_at, axis=1)
        return lax.dynamic_slice_in_dim(group_row, delay_at.astype(jnp.int32), sample_extent, axis=1)
    pulled = jax.vmap(spread, in_axes=(0, 0), out_axes=1)(group_of, launch_lags)
    return (sorting_choice.astype(jnp.float32) - correction_pace * pulled).astype(jnp.bfloat16)

def reference(initial_guess, measured_mixtures, launch_lags, source_launch_order, station_portion_tallies, source_entry_kernel, source_spaced_kernel, source_exit_kernel, source_inner_offsets, station_entry_kernel, station_spaced_kernel, station_exit_kernel, station_inner_offsets, learned_pace_factors):
    shot_count, recv_all, full_len = initial_guess.shape
    block_size = recv_all // N_LINE
    offsets, owner_of = sections(station_portion_tallies, block_size)
    shot_weights = (source_entry_kernel, source_spaced_kernel, source_exit_kernel, source_inner_offsets)
    receiver_weights = (station_entry_kernel, station_spaced_kernel, station_exit_kernel, station_inner_offsets)
    measured_mixtures_here = jnp.transpose(measured_mixtures, (1, 0, 2))
    ballot = (owner_of[:, None] == jnp.arange(station_portion_tallies.shape[0], dtype=jnp.int32)[None, :]).astype(jnp.float32)

    def shot_network(shot_traces):
        line_grid = shot_traces.reshape(LINES, RPL, full_len)
        edged_set = jnp.pad(line_grid, ((1, 1), (0, 0), (0, 0)))
        stacked = jnp.stack([edged_set[channel:channel + LINES] for channel in range(3)], axis=2)
        inputs = jnp.pad(stacked.reshape(recv_all, 3, full_len), ((0, 0), (0, 0), (MARGIN, MARGIN)))
        correction = network(inputs, 0, full_len, *shot_weights)
        return (shot_traces.astype(jnp.float32) + correction).astype(jnp.bfloat16)
    current = initial_guess
    for unrolled_round_ordinal in range(ITERS):
        after_shot = lax.map(shot_network, current)
        sorting_choice = jnp.transpose(after_shot, (1, 0, 2))
        energy = lax.optimization_barrier(jnp.sum(jnp.square(sorting_choice.astype(jnp.float32)), axis=(1, 2)))
        blocks = energy.reshape(N_LINE, block_size)
        section_sum = jnp.dot(blocks, ballot, precision=lax.Precision.HIGHEST)
        denominator = (jnp.take(station_portion_tallies, owner_of) * (shot_count * full_len)).astype(jnp.float32)
        mean_power = jnp.take(section_sum, owner_of, axis=1) / denominator[None, :]
        rms_scale = jnp.sqrt(mean_power.reshape(recv_all) + EPSILON)
        sorting_choice = receiver_pass(sorting_choice, rms_scale, receiver_weights)
        sorting_choice = mixture_leftover(sorting_choice, measured_mixtures_here, source_launch_order, launch_lags, learned_pace_factors[unrolled_round_ordinal])
        current = jnp.transpose(sorting_choice, (1, 0, 2))
    return current
```

```python
import functools
import math

import jax
import jax.numpy as jnp
from jax import lax
from jax.experimental import pallas as pl
from jax.experimental.pallas import tpu as pltpu
from jax.sharding import PartitionSpec as P

RPL = 16
ITERS = 2
EPSILON = 1e-05
C = 8
PACK = 4
TAPS = (1, 2, 3, 0)
F32, BF16 = jnp.float32, jnp.bfloat16
AXES = ("shot", "line", "tm")


def ahead(x, k):
    edge = pltpu.roll(x[:k], C - 1, 1)
    edge = jnp.where(lax.broadcasted_iota(jnp.int32, edge.shape, 1) == C - 1, 0.0, edge)
    return edge if k == x.shape[0] else jnp.concatenate([x[k:], edge], axis=0)


def behind(x, k):
    edge = pltpu.roll(x[x.shape[0] - k :], 1, 1)
    edge = jnp.where(lax.broadcasted_iota(jnp.int32, edge.shape, 1) == 0, 0.0, edge)
    return edge if k == x.shape[0] else jnp.concatenate([edge, x[: x.shape[0] - k]], axis=0)


def even_lanes(shape):
    return lax.broadcasted_iota(jnp.int32, shape, len(shape) - 1) < shape[-1] // 2


def net(x, w_in, w_mid, w_out, bias, total):
    planes, _, lanes = x.shape
    rows = planes * C
    side = jnp.where(even_lanes(x.shape), ahead(x, 1), behind(x, 1))
    z = jnp.concatenate([x, side], axis=2).astype(BF16).reshape(rows, 2 * lanes)
    total[...] = jnp.zeros_like(total)
    wide = w_in.shape[2]

    def step(q, carry):
        h = jnp.dot(z, w_in[q], preferred_element_type=F32)
        h = jnp.maximum(h + bias[0:1, :], 0.0)
        cube = h.reshape(planes, C, wide)
        first = ahead(cube[:2], 2).reshape(2 * C, wide).astype(BF16)
        last = behind(cube[planes - 2 :], 2).reshape(2 * C, wide).astype(BF16)
        hb = h.astype(BF16)
        early = jnp.concatenate([last, hb[: rows - 2 * C]], axis=0)
        late = jnp.concatenate([hb[2 * C :], first], axis=0)
        g = jnp.dot(jnp.concatenate([early, hb, late], axis=1), w_mid[...], preferred_element_type=F32)
        g = jnp.maximum(g + bias[1:2, :], 0.0).astype(BF16)
        total[...] += jnp.dot(g, w_out[q], preferred_element_type=F32)
        return carry

    lax.fori_loop(0, w_in.shape[0], step, 0)
    y = total[...].reshape(planes, C, 2 * lanes)
    a, b = y[:, :, :lanes], y[:, :, lanes:]
    return a + jnp.where(even_lanes(b.shape), behind(b, 1), ahead(b, 1))


def shot_step(x, weights, member, out_ref, part_ref, total):
    y = (x + net(x, *weights, total)).astype(BF16)
    out_ref[...] = y
    y = y.astype(F32)
    energy = jnp.sum(jnp.sum(y * y, axis=0), axis=0, keepdims=True)
    sums = jnp.sum(member[...] * energy, axis=1, keepdims=True)
    part_ref[...] = jnp.broadcast_to(sums, part_ref.shape)


def shifted(buf, lag_ref, shots, forward):
    planes, lanes = buf.shape[1] // 2, buf.shape[3]
    shape = (planes, C, lanes)
    even = even_lanes(shape)
    per = lanes // 2 // shots
    lane_shot = lax.rem(lax.broadcasted_iota(jnp.int32, shape, 2), lanes // 2) // per
    out = jnp.zeros(shape, F32)
    for s in range(shots):
        lag = lag_ref[s]
        half, odd = lag // 2, lax.rem(lag, 2)
        at_even = half if forward else planes - half - odd
        at_odd = half + odd if forward else planes - half
        one = jnp.where(even, buf[odd, pl.ds(at_even, planes)], buf[odd, pl.ds(at_odd, planes)])
        out = jnp.where(lane_shot == s, one, out)
    return out


def station_step(shots, sp, tot_ref, spread, weights, lags, join, mix, take, pace, buf, total):
    planes, _, lanes = sp.shape
    rows = planes * C
    mean = jnp.sum(tot_ref[:, 0:1] * spread[...], axis=0, keepdims=True)
    rms = jnp.sqrt(mean + EPSILON).reshape(1, 1, lanes)
    normed = (sp / rms).astype(BF16).astype(F32)
    settled = (sp + rms * net(normed, *weights, total)).astype(BF16).astype(F32)

    def fill(x, forward):
        far = ahead(x, planes) if forward else behind(x, planes)
        near_at, far_at = (0, planes) if forward else (planes, 0)
        for v, at in ((x, near_at), (far, far_at)):
            buf[0, at : at + planes] = v
            h = lanes // 2
            buf[1, at : at + planes] = jnp.concatenate([v[:, :, h:], v[:, :, :h]], axis=2)

    fill(settled, False)
    fired = shifted(buf, lags, shots, False).astype(BF16).reshape(rows, lanes)
    misfit = jnp.dot(fired, join[...], preferred_element_type=F32)
    misfit -= jnp.dot(mix[...], take[...], preferred_element_type=F32)
    fill(misfit.reshape(planes, C, lanes), True)
    return (settled - pace * shifted(buf, lags, shots, True)).astype(BF16)


def first_kernel(x, wi, wm, wo, bi, member, out, part, total):
    shot_step(x[...].astype(F32), (wi, wm, wo, bi), member, out, part, total)


def station_kernel(it, shots, lags, pace, sp, tot, spread, wi, wm, wo, bi, join, mix, take, out, buf, total):
    out[...] = station_step(
        shots, sp[...].astype(F32), tot, spread, (wi, wm, wo, bi), lags, join, mix, take, pace[it], buf, total
    )


def both_kernel(
    it, shots, lags, pace, sp, tot, spread, wi, wm, wo, bi, join, mix, take, vi, vm, vo, ci, member, out, part, buf, total
):
    x = station_step(
        shots, sp[...].astype(F32), tot, spread, (wi, wm, wo, bi), lags, join, mix, take, pace[it], buf, total
    )
    shot_step(x.astype(F32), (vi, vm, vo, ci), member, out, part, total)


def call(body, outs, ins, smem, scratch):
    v, s = pl.BlockSpec(memory_space=pltpu.VMEM), pl.BlockSpec(memory_space=pltpu.SMEM)
    return pl.pallas_call(
        body,
        out_shape=outs,
        in_specs=[s] * smem + [v] * (len(ins) - smem),
        out_specs=jax.tree.map(lambda _: v, outs),
        scratch_shapes=scratch,
        compiler_params=pltpu.CompilerParams(vmem_limit_bytes=48 * 2**20),
    )(*ins)


def prepared(w_in, w_mid, w_out, bias, near):
    n, feat = near.shape[1], w_in.shape[2]
    tiles = n // PACK
    near, own = near.astype(BF16), jnp.eye(n, dtype=BF16)
    w1 = jnp.stack([w_in[j] for j in TAPS])
    cols = near.reshape(3, n, tiles, PACK).transpose(0, 2, 1, 3)
    big = sum(w1[:, None, None, None, c, :] * cols[c][None, :, :, :, None] for c in range(3))
    big = big.transpose(1, 0, 2, 3, 4).reshape(tiles, 4 * n, PACK * feat)
    eye = jnp.eye(PACK, dtype=BF16)
    mid = (w_mid[:, None, :, None, :] * eye[None, :, None, :, None]).reshape(3 * PACK * feat, PACK * feat)
    w2 = jnp.stack([w_out[k] for k in TAPS])
    out = w2.T[None, None, :, :, None] * own.reshape(tiles, PACK, 1, 1, n)
    return big, mid, out.reshape(tiles, PACK * feat, 4 * n), jnp.tile(bias, (1, PACK))


def per_device(guess, mixtures, lags, order, tallies, e1, m1, x1, b1, e2, m2, x2, b2, pace):
    sh, recv, tl = guess.shape
    n_shot, n_line, n_tm = (lax.axis_size(a) for a in AXES)
    whole = RPL % (n_shot * n_line * n_tm) == 0
    where = AXES if whole else AXES[1:]
    parts = math.prod(lax.axis_size(a) for a in where)
    kp, lh = RPL // parts, recv // RPL
    lines, shots, nt = lh * n_line, sh * n_shot, tl * n_tm
    planes, s1 = nt // 2 // C, shots if whole else sh
    r1 = lines * kp
    r2 = r1 if whole else r1 // n_shot
    lanes1, lanes2 = 2 * s1 * r1, 2 * shots * r2
    sources = n_shot if whole else 1
    i32 = functools.partial(jnp.arange, dtype=jnp.int32)

    x = guess.reshape(sh, lh, parts, kp, tl).transpose(2, 0, 1, 3, 4)
    x = lax.all_to_all(x, where, split_axis=0, concat_axis=0)
    x = x.reshape(sources, n_line, n_tm, sh, lh, kp, tl).transpose(0, 3, 1, 4, 5, 2, 6)
    x = x.reshape(s1, r1, C, planes, 2).transpose(3, 2, 4, 0, 1).reshape(planes, C, lanes1)

    at_shot = lax.axis_index("shot")

    def first_k(line):
        block = line * n_tm + lax.axis_index("tm")
        return (at_shot * n_line * n_tm + block if whole else block) * kp

    n_mix = mixtures.shape[0]
    grid = mixtures.reshape(n_mix, lh, RPL, nt)
    sent = jnp.stack([lax.dynamic_slice_in_dim(grid, first_k(d), kp, axis=2) for d in range(n_line)])
    m = lax.all_to_all(sent, "line", split_axis=0, concat_axis=0)
    m = m.transpose(1, 0, 2, 3, 4).reshape(n_mix, r1, nt)
    if not whole:
        m = lax.dynamic_slice_in_dim(m, at_shot * r2, r2, axis=1)
    m = m.reshape(n_mix, r2, C, planes, 2).transpose(3, 2, 4, 0, 1).reshape(planes * C, 2 * n_mix * r2)

    np_ = tallies.shape[0]
    here = i32(np_)
    offsets = jnp.sum(jnp.where(here[None, :] < here[:, None], tallies[None, :], 0), axis=1)
    mine = first_k(lax.axis_index("line"))

    def one_hot(r):
        line, k = r // kp, mine + lax.rem(r, kp)
        q = lax.rem(line, lh) * RPL + k
        inside = (offsets[:, None] <= q[None, :]) & (q[None, :] < (offsets + tallies)[:, None])
        block = (line // lh)[None, :] == i32(n_line)[:, None]
        return (block[:, None, :] & inside[None, :, :]).reshape(n_line * np_, r.shape[0]).astype(F32)

    member = jnp.tile(one_hot(i32(r1)), (1, 2 * s1))
    r_own = i32(r2) if whole else at_shot * r2 + i32(r2)
    count = jnp.tile((tallies * (shots * nt)).astype(F32), n_line)
    spread = jnp.tile(one_hot(r_own) / count[:, None], (1, 2 * shots))

    sid = i32(shots)
    place = jnp.sum(jnp.where(order[None, :] == sid[:, None], sid[None, :], 0), axis=1)
    group = place // (shots // n_mix)
    same = (group[:, None] == group[None, :]).astype(BF16)
    chosen = (i32(n_mix)[:, None] == group[None, :]).astype(BF16)
    rest, two = jnp.eye(r2, dtype=BF16), jnp.eye(2, dtype=BF16)
    join = jnp.kron(two, jnp.kron(same, rest))
    take = jnp.kron(two, jnp.kron(chosen, rest))

    n1, n2 = s1 * r1, shots * r2
    a, b = i32(n1)[:, None], i32(n1)[None, :]
    near1 = jnp.stack([(a == b + (c - 1) * kp) & (a // r1 == b // r1) for c in range(3)])
    a, b = i32(n2)[:, None], i32(n2)[None, :]
    near2 = jnp.stack([a == b + (c - 1) * r2 for c in range(3)])
    wa = prepared(e1, m1, x1, b1, near1)
    wb = prepared(e2, m2, x2, b2, near2)

    rows = planes * C
    tot1, tot2 = pltpu.VMEM((rows, 2 * lanes1), F32), pltpu.VMEM((rows, 2 * lanes2), F32)
    buf = pltpu.VMEM((2, 2 * planes, C, lanes2), F32)
    spass = jax.ShapeDtypeStruct((planes, C, lanes1), BF16)
    part = jax.ShapeDtypeStruct((n_line * np_, 128), F32)
    moved = jax.ShapeDtypeStruct((planes, C, lanes2), BF16)

    def to_stations(y):
        y = y.reshape(rows, 2, sh, n_shot, r2)
        y = lax.all_to_all(y, "shot", split_axis=3, concat_axis=2, tiled=True)
        return y.reshape(planes, C, lanes2)

    def to_shots(y):
        y = y.reshape(rows, 2, shots, 1, r2)
        y = lax.all_to_all(y, "shot", split_axis=2, concat_axis=3, tiled=True)
        return y.reshape(planes, C, lanes1)

    sp, energy = call(first_kernel, (spass, part), (x, *wa, member), 0, [tot1])
    for it in range(ITERS):
        tot = lax.psum(energy, AXES)
        if not whole:
            sp = to_stations(sp)
        ins = (lags, pace, sp, tot, spread, *wb, join, m, take)
        if whole and it < ITERS - 1:
            sp, energy = call(
                functools.partial(both_kernel, it, shots), (spass, part), (*ins, *wa, member), 2, [buf, tot2]
            )
            continue
        x = call(functools.partial(station_kernel, it, shots), moved, ins, 2, [buf, tot2])
        if not whole:
            x = to_shots(x)
            if it < ITERS - 1:
                sp, energy = call(first_kernel, (spass, part), (x, *wa, member), 0, [tot1])

    x = x.reshape(planes, C, 2, s1, r1).transpose(3, 4, 1, 0, 2)
    x = x.reshape(sources, sh, n_line, lh, kp, n_tm, tl).transpose(0, 2, 5, 1, 3, 4, 6)
    x = lax.all_to_all(x.reshape(parts, sh, lh, kp, tl), where, split_axis=0, concat_axis=0)
    return x.transpose(1, 2, 0, 3, 4).reshape(sh, recv, tl)


def solution(mesh):
    spec = P(("group", "shot"), "line", "tm")
    placed = (spec, P("group", "line", None), P("group"), P("group"), P("group")) + (P(),) * 9
    return jax.shard_map(per_device, mesh=mesh, in_specs=placed, out_specs=spec, check_vma=False)
```

```python
import functools
import math

import jax
import jax.numpy as jnp
import numpy as np
from jax import lax
from jax.experimental import pallas as pl
from jax.experimental.pallas import tpu as pltpu
from jax.sharding import PartitionSpec as P

RPL = 16
ITERS = 2
EPSILON = 1e-05
C = 8
PACK = 4
TAPS = (1, 2, 3, 0)
F32, BF16 = jnp.float32, jnp.bfloat16
AXES = ("shot", "line", "tm")


def ahead(x, k):
    edge = pltpu.roll(x[:k], C - 1, 1)
    edge = jnp.where(lax.broadcasted_iota(jnp.int32, edge.shape, 1) == C - 1, 0.0, edge)
    return edge if k == x.shape[0] else jnp.concatenate([x[k:], edge], axis=0)


def behind(x, k):
    edge = pltpu.roll(x[x.shape[0] - k :], 1, 1)
    edge = jnp.where(lax.broadcasted_iota(jnp.int32, edge.shape, 1) == 0, 0.0, edge)
    return edge if k == x.shape[0] else jnp.concatenate([edge, x[: x.shape[0] - k]], axis=0)


def even_lanes(shape):
    return lax.broadcasted_iota(jnp.int32, shape, len(shape) - 1) < shape[-1] // 2


def net(x, w_in, pick, w_mid, w_out, place, bias, total, band):
    planes, _, lanes = x.shape
    rows = planes * C
    side = jnp.where(even_lanes(x.shape), ahead(x, 1), behind(x, 1))
    z = jnp.concatenate([x, side], axis=2).astype(BF16).reshape(rows, 2 * lanes)
    total[...] = jnp.zeros_like(total)
    wide = w_in.shape[1]
    feat = wide // PACK
    for j in range(3):
        tap = w_mid[j].astype(F32)
        for i in range(PACK):
            row = [tap if p == i else jnp.zeros_like(tap) for p in range(PACK)]
            at = (j * PACK + i) * feat
            band[at : at + feat, :] = jnp.concatenate(row, axis=1).astype(BF16)

    def step(q, carry):
        w_here = jnp.dot(pick[q], w_in[...], preferred_element_type=F32).astype(BF16)
        o_here = jnp.dot(w_out[...], place[q], preferred_element_type=F32).astype(BF16)
        h = jnp.dot(z, w_here, preferred_element_type=F32)
        h = jnp.maximum(h + bias[0:1, :], 0.0)
        cube = h.reshape(planes, C, wide)
        first = ahead(cube[:2], 2).reshape(2 * C, wide).astype(BF16)
        last = behind(cube[planes - 2 :], 2).reshape(2 * C, wide).astype(BF16)
        hb = h.astype(BF16)
        early = jnp.concatenate([last, hb[: rows - 2 * C]], axis=0)
        late = jnp.concatenate([hb[2 * C :], first], axis=0)
        g = jnp.dot(jnp.concatenate([early, hb, late], axis=1), band[...], preferred_element_type=F32)
        g = jnp.maximum(g + bias[1:2, :], 0.0).astype(BF16)
        total[...] += jnp.dot(g, o_here, preferred_element_type=F32)
        return carry

    lax.fori_loop(0, pick.shape[0], step, 0)
    y = total[...].reshape(planes, C, 2 * lanes)
    a, b = y[:, :, :lanes], y[:, :, lanes:]
    return a + jnp.where(even_lanes(b.shape), behind(b, 1), ahead(b, 1))


def shot_step(x, weights, member, out_ref, part_ref, total, band):
    y = (x + net(x, *weights, total, band)).astype(BF16)
    out_ref[...] = y
    y = y.astype(F32)
    energy = jnp.sum(jnp.sum(y * y, axis=0), axis=0, keepdims=True)
    sums = jnp.sum(member[...] * energy, axis=1, keepdims=True)
    part_ref[...] = jnp.broadcast_to(sums, part_ref.shape)


def shifted(buf, lag_ref, shots, forward):
    planes, lanes = buf.shape[1] // 2, buf.shape[3]
    shape = (planes, C, lanes)
    even = even_lanes(shape)
    per = lanes // 2 // shots
    lane_shot = lax.rem(lax.broadcasted_iota(jnp.int32, shape, 2), lanes // 2) // per
    out = jnp.zeros(shape, F32)
    for s in range(shots):
        lag = lag_ref[s]
        half, odd = lag // 2, lax.rem(lag, 2)
        at_even = half if forward else planes - half - odd
        at_odd = half + odd if forward else planes - half
        one = jnp.where(even, buf[odd, pl.ds(at_even, planes)], buf[odd, pl.ds(at_odd, planes)])
        out = jnp.where(lane_shot == s, one, out)
    return out


def station_step(shots, sp, tot_ref, spread, weights, lags, join, mix, take, pace, buf, total, band):
    planes, _, lanes = sp.shape
    rows = planes * C
    mean = jnp.sum(tot_ref[:, 0:1] * spread[...], axis=0, keepdims=True)
    rms = jnp.sqrt(mean + EPSILON).reshape(1, 1, lanes)
    normed = (sp / rms).astype(BF16).astype(F32)
    settled = (sp + rms * net(normed, *weights, total, band)).astype(BF16).astype(F32)

    def fill(x, forward):
        far = ahead(x, planes) if forward else behind(x, planes)
        near_at, far_at = (0, planes) if forward else (planes, 0)
        for v, at in ((x, near_at), (far, far_at)):
            buf[0, at : at + planes] = v
            h = lanes // 2
            buf[1, at : at + planes] = jnp.concatenate([v[:, :, h:], v[:, :, :h]], axis=2)

    fill(settled, False)
    fired = shifted(buf, lags, shots, False).astype(BF16).reshape(rows, lanes)
    misfit = jnp.dot(fired, join[...], preferred_element_type=F32)
    misfit -= jnp.dot(mix[...], take[...], preferred_element_type=F32)
    fill(misfit.reshape(planes, C, lanes), True)
    return (settled - pace * shifted(buf, lags, shots, True)).astype(BF16)


def first_kernel(x, wi, wp, wm, wo, wq, bi, member, out, part, total, band):
    shot_step(x[...].astype(F32), (wi, wp, wm, wo, wq, bi), member, out, part, total, band)


def station_kernel(it, shots, lags, pace, sp, tot, spread, wi, wp, wm, wo, wq, bi, join, mix, take, out, buf, total, band):
    out[...] = station_step(
        shots, sp[...].astype(F32), tot, spread, (wi, wp, wm, wo, wq, bi), lags, join, mix, take, pace[it], buf, total, band
    )


def both_kernel(
    it, shots, lags, pace, sp, tot, spread, wi, wp, wm, wo, wq, bi, join, mix, take, vi, vp, vm, vo, vq, ci, member, out, part, buf, total, band
):
    x = station_step(
        shots, sp[...].astype(F32), tot, spread, (wi, wp, wm, wo, wq, bi), lags, join, mix, take, pace[it], buf, total, band
    )
    shot_step(x.astype(F32), (vi, vp, vm, vo, vq, ci), member, out, part, total, band)


def call(body, outs, ins, smem, scratch):
    v, s = pl.BlockSpec(memory_space=pltpu.VMEM), pl.BlockSpec(memory_space=pltpu.SMEM)
    return pl.pallas_call(
        body,
        out_shape=outs,
        in_specs=[s] * smem + [v] * (len(ins) - smem),
        out_specs=jax.tree.map(lambda _: v, outs),
        scratch_shapes=scratch,
        compiler_params=pltpu.CompilerParams(vmem_limit_bytes=48 * 2**20),
    )(*ins)


def prepared(w_in, w_mid, w_out, bias, near):
    n, feat = near.shape[1], w_in.shape[2]
    tiles = n // PACK
    cols = near.reshape(3, n, tiles, PACK).transpose(2, 1, 0, 3)
    pick = np.einsum("jk,tnci->tjnkci", np.eye(4), cols).reshape(tiles, 4 * n, 12 * PACK)
    place = np.einsum("jk,tin->tjikn", np.eye(4), np.eye(n).reshape(tiles, PACK, n)).reshape(tiles, 4 * PACK, 4 * n)
    w1 = jnp.stack([w_in[j] for j in TAPS]).reshape(12, 1, 1, feat)
    eye = jnp.eye(PACK, dtype=BF16)
    rows = (w1 * eye[None, :, :, None]).reshape(12 * PACK, PACK * feat)
    w2 = jnp.stack([w_out[k] for k in TAPS]).T.reshape(1, feat, 4, 1)
    ends = (w2 * eye[:, None, None, :]).reshape(PACK * feat, 4 * PACK)
    return rows, jnp.asarray(pick, BF16), w_mid, ends, jnp.asarray(place, BF16), jnp.tile(bias, (1, PACK))


def exchange_kernel(sizes, x, out, slots, send, recv):
    count = math.prod(sizes)
    me = (lax.axis_index("shot") * sizes[1] + lax.axis_index("line")) * sizes[2] + lax.axis_index("tm")

    def peer(off):
        at = lax.rem(me + off, count)
        return {
            "shot": at // (sizes[1] * sizes[2]),
            "line": lax.rem(at // sizes[2], sizes[1]),
            "tm": lax.rem(at, sizes[2]),
        }

    barrier = pltpu.get_barrier_semaphore()
    for off in range(1, count):
        pl.semaphore_signal(barrier, inc=1, device_id=peer(off), device_id_type=pl.DeviceIdType.MESH)
    pl.semaphore_wait(barrier, count - 1)
    copies = []
    for off in range(1, count):
        copy = pltpu.make_async_remote_copy(
            src_ref=x,
            dst_ref=slots.at[off],
            send_sem=send.at[off],
            recv_sem=recv.at[off],
            device_id=peer(off),
            device_id_type=pl.DeviceIdType.MESH,
        )
        copy.start()
        copies.append(copy)
    total = x[...]
    for off, copy in enumerate(copies, 1):
        copy.wait()
        total += slots[off]
    out[...] = total


def summed(x, sizes):
    count, v = math.prod(sizes), pl.BlockSpec(memory_space=pltpu.VMEM)
    return pl.pallas_call(
        functools.partial(exchange_kernel, sizes),
        out_shape=jax.ShapeDtypeStruct(x.shape, x.dtype),
        in_specs=[v],
        out_specs=v,
        scratch_shapes=[
            pltpu.VMEM((count, *x.shape), x.dtype),
            pltpu.SemaphoreType.DMA((count,)),
            pltpu.SemaphoreType.DMA((count,)),
        ],
        compiler_params=pltpu.CompilerParams(collective_id=0, has_side_effects=True),
    )(x)


def per_device(guess, mixtures, lags, order, tallies, e1, m1, x1, b1, e2, m2, x2, b2, pace):
    sh, recv, tl = guess.shape
    n_shot, n_line, n_tm = (lax.axis_size(a) for a in AXES)
    whole = RPL % (n_shot * n_line * n_tm) == 0
    where = AXES if whole else AXES[1:]
    parts = math.prod(lax.axis_size(a) for a in where)
    kp, lh = RPL // parts, recv // RPL
    lines, shots, nt = lh * n_line, sh * n_shot, tl * n_tm
    planes, s1 = nt // 2 // C, shots if whole else sh
    r1 = lines * kp
    r2 = r1 if whole else r1 // n_shot
    lanes1, lanes2 = 2 * s1 * r1, 2 * shots * r2
    sources = n_shot if whole else 1
    i32 = functools.partial(jnp.arange, dtype=jnp.int32)

    x = guess.reshape(sh, lh, parts, kp, tl).transpose(2, 0, 1, 3, 4)
    x = lax.all_to_all(x, where, split_axis=0, concat_axis=0)
    x = x.reshape(sources, n_line, n_tm, sh, lh, kp, tl).transpose(0, 3, 1, 4, 5, 2, 6)
    x = x.reshape(s1, r1, C, planes, 2).transpose(3, 2, 4, 0, 1).reshape(planes, C, lanes1)

    at_shot = lax.axis_index("shot")

    def first_k(line):
        block = line * n_tm + lax.axis_index("tm")
        return (at_shot * n_line * n_tm + block if whole else block) * kp

    n_mix = mixtures.shape[0]
    grid = mixtures.reshape(n_mix, lh, RPL, nt)
    sent = jnp.stack([lax.dynamic_slice_in_dim(grid, first_k(d), kp, axis=2) for d in range(n_line)])
    m = lax.all_to_all(sent, "line", split_axis=0, concat_axis=0)
    m = m.transpose(1, 0, 2, 3, 4).reshape(n_mix, r1, nt)
    if not whole:
        m = lax.dynamic_slice_in_dim(m, at_shot * r2, r2, axis=1)
    m = m.reshape(n_mix, r2, C, planes, 2).transpose(3, 2, 4, 0, 1).reshape(planes * C, 2 * n_mix * r2)

    np_ = tallies.shape[0]
    here = i32(np_)
    offsets = jnp.sum(jnp.where(here[None, :] < here[:, None], tallies[None, :], 0), axis=1)
    mine = first_k(lax.axis_index("line"))

    def one_hot(r):
        line, k = r // kp, mine + lax.rem(r, kp)
        q = lax.rem(line, lh) * RPL + k
        inside = (offsets[:, None] <= q[None, :]) & (q[None, :] < (offsets + tallies)[:, None])
        block = (line // lh)[None, :] == i32(n_line)[:, None]
        return (block[:, None, :] & inside[None, :, :]).reshape(n_line * np_, r.shape[0]).astype(F32)

    member = jnp.tile(one_hot(i32(r1)), (1, 2 * s1))
    r_own = i32(r2) if whole else at_shot * r2 + i32(r2)
    count = jnp.tile((tallies * (shots * nt)).astype(F32), n_line)
    spread = jnp.tile(one_hot(r_own) / count[:, None], (1, 2 * shots))

    sid = i32(shots)
    place = jnp.sum(jnp.where(order[None, :] == sid[:, None], sid[None, :], 0), axis=1)
    group = place // (shots // n_mix)
    same = (group[:, None] == group[None, :]).astype(BF16)
    chosen = (i32(n_mix)[:, None] == group[None, :]).astype(BF16)
    rest, two = jnp.eye(r2, dtype=BF16), jnp.eye(2, dtype=BF16)
    join = jnp.kron(two, jnp.kron(same, rest))
    take = jnp.kron(two, jnp.kron(chosen, rest))

    n1, n2 = s1 * r1, shots * r2
    a, b = np.arange(n1)[:, None], np.arange(n1)[None, :]
    near1 = np.stack([(a == b + (c - 1) * kp) & (a // r1 == b // r1) for c in range(3)])
    a, b = np.arange(n2)[:, None], np.arange(n2)[None, :]
    near2 = np.stack([a == b + (c - 1) * r2 for c in range(3)])
    wa = prepared(e1, m1, x1, b1, near1)
    wb = prepared(e2, m2, x2, b2, near2)

    rows = planes * C
    tot1, tot2 = pltpu.VMEM((rows, 2 * lanes1), F32), pltpu.VMEM((rows, 2 * lanes2), F32)
    feat = e1.shape[2]
    band = pltpu.VMEM((3 * PACK * feat, PACK * feat), BF16)
    buf = pltpu.VMEM((2, 2 * planes, C, lanes2), F32)
    spass = jax.ShapeDtypeStruct((planes, C, lanes1), BF16)
    part = jax.ShapeDtypeStruct((n_line * np_, 128), F32)
    moved = jax.ShapeDtypeStruct((planes, C, lanes2), BF16)

    def to_stations(y):
        y = y.reshape(rows, 2, sh, n_shot, r2)
        y = lax.all_to_all(y, "shot", split_axis=3, concat_axis=2, tiled=True)
        return y.reshape(planes, C, lanes2)

    def to_shots(y):
        y = y.reshape(rows, 2, shots, 1, r2)
        y = lax.all_to_all(y, "shot", split_axis=2, concat_axis=3, tiled=True)
        return y.reshape(planes, C, lanes1)

    sp, energy = call(first_kernel, (spass, part), (x, *wa, member), 0, [tot1, band])
    for it in range(ITERS):
        tot = summed(energy, (n_shot, n_line, n_tm)) if whole else lax.psum(energy, AXES)
        if not whole:
            sp = to_stations(sp)
        ins = (lags, pace, sp, tot, spread, *wb, join, m, take)
        if whole and it < ITERS - 1:
            sp, energy = call(
                functools.partial(both_kernel, it, shots), (spass, part), (*ins, *wa, member), 2, [buf, tot2, band]
            )
            continue
        x = call(functools.partial(station_kernel, it, shots), moved, ins, 2, [buf, tot2, band])
        if not whole:
            x = to_shots(x)
            if it < ITERS - 1:
                sp, energy = call(first_kernel, (spass, part), (x, *wa, member), 0, [tot1, band])

    x = x.reshape(planes, C, 2, s1, r1).transpose(3, 4, 1, 0, 2)
    x = x.reshape(sources, sh, n_line, lh, kp, n_tm, tl).transpose(0, 2, 5, 1, 3, 4, 6)
    x = lax.all_to_all(x.reshape(parts, sh, lh, kp, tl), where, split_axis=0, concat_axis=0)
    return x.transpose(1, 2, 0, 3, 4).reshape(sh, recv, tl)


def solution(mesh):
    spec = P(("group", "shot"), "line", "tm")
    placed = (spec, P("group", "line", None), P("group"), P("group"), P("group")) + (P(),) * 9
    return jax.shard_map(per_device, mesh=mesh, in_specs=placed, out_specs=spec, check_vma=False)
```

```python
import functools
import math

import jax
import jax.numpy as jnp
import numpy as np
from jax import lax
from jax.experimental import pallas as pl
from jax.experimental.pallas import tpu as pltpu
from jax.sharding import PartitionSpec as P

RPL = 16
ITERS = 2
EPSILON = 1e-05
C = 8
PACK = 4
TAPS = (1, 2, 3, 0)
F32, BF16 = jnp.float32, jnp.bfloat16
AXES = ("shot", "line", "tm")


def ahead(x, k):
    edge = pltpu.roll(x[:k], C - 1, 1)
    edge = jnp.where(lax.broadcasted_iota(jnp.int32, edge.shape, 1) == C - 1, 0.0, edge)
    return edge if k == x.shape[0] else jnp.concatenate([x[k:], edge], axis=0)


def behind(x, k):
    edge = pltpu.roll(x[x.shape[0] - k :], 1, 1)
    edge = jnp.where(lax.broadcasted_iota(jnp.int32, edge.shape, 1) == 0, 0.0, edge)
    return edge if k == x.shape[0] else jnp.concatenate([edge, x[: x.shape[0] - k]], axis=0)


def even_lanes(shape):
    return lax.broadcasted_iota(jnp.int32, shape, len(shape) - 1) < shape[-1] // 2


def net(x, w_in, pick, w_mid, w_out, place, bias, total, band):
    planes, _, lanes = x.shape
    rows = planes * C
    side = jnp.where(even_lanes(x.shape), ahead(x, 1), behind(x, 1))
    z = jnp.concatenate([x, side], axis=2).astype(BF16).reshape(rows, 2 * lanes)
    total[...] = jnp.zeros_like(total)
    wide = w_in.shape[1]
    feat = wide // PACK
    for j in range(3):
        tap = w_mid[j].astype(F32)
        for i in range(PACK):
            row = [tap if p == i else jnp.zeros_like(tap) for p in range(PACK)]
            at = (j * PACK + i) * feat
            band[at : at + feat, :] = jnp.concatenate(row, axis=1).astype(BF16)

    def step(q, carry):
        w_here = jnp.dot(pick[q], w_in[...], preferred_element_type=F32).astype(BF16)
        o_here = jnp.dot(w_out[...], place[q], preferred_element_type=F32).astype(BF16)
        h = jnp.dot(z, w_here, preferred_element_type=F32)
        h = jnp.maximum(h + bias[0:1, :], 0.0)
        cube = h.reshape(planes, C, wide)
        first = ahead(cube[:2], 2).reshape(2 * C, wide).astype(BF16)
        last = behind(cube[planes - 2 :], 2).reshape(2 * C, wide).astype(BF16)
        hb = h.astype(BF16)
        early = jnp.concatenate([last, hb[: rows - 2 * C]], axis=0)
        late = jnp.concatenate([hb[2 * C :], first], axis=0)
        g = jnp.dot(jnp.concatenate([early, hb, late], axis=1), band[...], preferred_element_type=F32)
        g = jnp.maximum(g + bias[1:2, :], 0.0).astype(BF16)
        total[...] += jnp.dot(g, o_here, preferred_element_type=F32)
        return carry

    lax.fori_loop(0, pick.shape[0], step, 0, unroll=2)
    y = total[...].reshape(planes, C, 2 * lanes)
    a, b = y[:, :, :lanes], y[:, :, lanes:]
    return a + jnp.where(even_lanes(b.shape), behind(b, 1), ahead(b, 1))


def shot_step(x, weights, member, out_ref, part_ref, total, band):
    y = (x + net(x, *weights, total, band)).astype(BF16)
    out_ref[...] = y
    y = y.astype(F32)
    energy = jnp.sum(jnp.sum(y * y, axis=0), axis=0, keepdims=True)
    sums = jnp.sum(member[...] * energy, axis=1, keepdims=True)
    part_ref[...] = jnp.broadcast_to(sums, part_ref.shape)


def shifted(buf, lag_ref, shots, forward):
    planes, lanes = buf.shape[1] // 2, buf.shape[3]
    shape = (planes, C, lanes)
    even = even_lanes(shape)
    per = lanes // 2 // shots
    lane_shot = lax.rem(lax.broadcasted_iota(jnp.int32, shape, 2), lanes // 2) // per
    out = jnp.zeros(shape, F32)
    for s in range(shots):
        lag = lag_ref[s]
        half, odd = lag // 2, lax.rem(lag, 2)
        at_even = half if forward else planes - half - odd
        at_odd = half + odd if forward else planes - half
        one = jnp.where(even, buf[odd, pl.ds(at_even, planes)], buf[odd, pl.ds(at_odd, planes)])
        out = jnp.where(lane_shot == s, one, out)
    return out


def station_step(shots, sp, tot_ref, spread, weights, lags, join, mix, take, pace, buf, total, band):
    planes, _, lanes = sp.shape
    rows = planes * C
    mean = jnp.sum(tot_ref[:, 0:1] * spread[...], axis=0, keepdims=True)
    rms = jnp.sqrt(mean + EPSILON).reshape(1, 1, lanes)
    normed = (sp / rms).astype(BF16).astype(F32)
    settled = (sp + rms * net(normed, *weights, total, band)).astype(BF16).astype(F32)

    def fill(x, forward):
        far = ahead(x, planes) if forward else behind(x, planes)
        near_at, far_at = (0, planes) if forward else (planes, 0)
        for v, at in ((x, near_at), (far, far_at)):
            buf[0, at : at + planes] = v
            h = lanes // 2
            buf[1, at : at + planes] = jnp.concatenate([v[:, :, h:], v[:, :, :h]], axis=2)

    fill(settled, False)
    fired = shifted(buf, lags, shots, False).astype(BF16).reshape(rows, lanes)
    misfit = jnp.dot(fired, join[...], preferred_element_type=F32)
    misfit -= jnp.dot(mix[...], take[...], preferred_element_type=F32)
    fill(misfit.reshape(planes, C, lanes), True)
    return (settled - pace * shifted(buf, lags, shots, True)).astype(BF16)


def by_phase(width):
    row = lax.broadcasted_iota(jnp.int32, (width, width), 0)
    col = lax.broadcasted_iota(jnp.int32, (width, width), 1)
    half = width // 2
    return jnp.where(col == 2 * lax.rem(row, half) + row // half, 1.0, 0.0).astype(BF16)


def unfold(read, into, sort):
    planes = into.shape[0]
    for c in range(C):
        v = lax.dot_general(sort, read(c), (((1,), (1,)), ((), ())), preferred_element_type=F32)
        into[:, c, :] = jnp.concatenate([v[:planes], v[planes:]], axis=1)


def entry_kernel(
    dims, x, m, wi, wp, wm, wo, wq, bi, member, out, part, mix, total, band, cube, side
):
    shots, blocks, halves = dims
    width = 2 * cube.shape[0]
    sort, each = by_phase(width), C // halves

    def traces(c):
        at, t = slice(c % each * width, (c % each + 1) * width), c // each
        rows = [x[(s * blocks + b) * halves + t, :, at].astype(F32) for s in range(shots) for b in range(blocks)]
        return jnp.concatenate(rows, axis=0).astype(BF16)

    def records(c):
        at = slice(c * width, (c + 1) * width)
        rows = [m[b, g, :, at].astype(F32) for g in range(m.shape[1]) for b in range(blocks)]
        return jnp.concatenate(rows, axis=0).astype(BF16)

    unfold(records, side, sort)
    mix[...] = side[...].astype(BF16).reshape(mix.shape)
    unfold(traces, cube, sort)
    shot_step(cube[...], (wi, wp, wm, wo, wq, bi), member, out, part, total, band)


def exit_kernel(
    it, dims, lags, pace, sp, tot, spread, wi, wp, wm, wo, wq, bi, join, mix, take, out, buf, total, band, cube
):
    shots, blocks, halves = dims
    width = 2 * cube.shape[0]
    sort, each = by_phase(width), C // halves
    x = station_step(
        shots, sp[...].astype(F32), tot, spread, (wi, wp, wm, wo, wq, bi), lags, join, mix, take, pace[it], buf, total, band
    )
    cube[...] = x.astype(F32)
    n, lh = cube.shape[2] // 2, out.shape[1]
    for c in range(C):
        v = cube[:, c, :]
        v = jnp.concatenate([v[:, :n], v[:, n:]], axis=0).T.astype(BF16)
        v = jnp.dot(v, sort, preferred_element_type=F32)
        at, t = slice(c % each * width, (c % each + 1) * width), c // each
        for j in range(shots * blocks):
            out[j * halves + t, :, at] = v[j * lh : (j + 1) * lh].astype(BF16)


def first_kernel(x, wi, wp, wm, wo, wq, bi, member, out, part, total, band):
    shot_step(x[...].astype(F32), (wi, wp, wm, wo, wq, bi), member, out, part, total, band)


def station_kernel(it, shots, lags, pace, sp, tot, spread, wi, wp, wm, wo, wq, bi, join, mix, take, out, buf, total, band):
    out[...] = station_step(
        shots, sp[...].astype(F32), tot, spread, (wi, wp, wm, wo, wq, bi), lags, join, mix, take, pace[it], buf, total, band
    )


def both_kernel(
    it, shots, lags, pace, sp, tot, spread, wi, wp, wm, wo, wq, bi, join, mix, take, vi, vp, vm, vo, vq, ci, member, out, part, buf, total, band
):
    x = station_step(
        shots, sp[...].astype(F32), tot, spread, (wi, wp, wm, wo, wq, bi), lags, join, mix, take, pace[it], buf, total, band
    )
    shot_step(x.astype(F32), (vi, vp, vm, vo, vq, ci), member, out, part, total, band)


def call(body, outs, ins, smem, scratch):
    v, s = pl.BlockSpec(memory_space=pltpu.VMEM), pl.BlockSpec(memory_space=pltpu.SMEM)
    return pl.pallas_call(
        body,
        out_shape=outs,
        in_specs=[s] * smem + [v] * (len(ins) - smem),
        out_specs=jax.tree.map(lambda _: v, outs),
        scratch_shapes=scratch,
        compiler_params=pltpu.CompilerParams(vmem_limit_bytes=48 * 2**20),
    )(*ins)


def prepared(w_in, w_mid, w_out, bias, near):
    n, feat = near.shape[1], w_in.shape[2]
    tiles = n // PACK
    cols = near.reshape(3, n, tiles, PACK).transpose(2, 1, 0, 3)
    pick = np.einsum("jk,tnci->tjnkci", np.eye(4)[list(TAPS)], cols).reshape(tiles, 4 * n, 12 * PACK)
    place = np.einsum("kj,tin->tjikn", np.eye(4)[list(TAPS)], np.eye(n).reshape(tiles, PACK, n)).reshape(tiles, 4 * PACK, 4 * n)
    w1 = w_in.reshape(12, 1, 1, feat)
    eye = jnp.eye(PACK, dtype=BF16)
    rows = (w1 * eye[None, :, :, None]).reshape(12 * PACK, PACK * feat)
    w2 = w_out.T.reshape(1, feat, 4, 1)
    ends = (w2 * eye[:, None, None, :]).reshape(PACK * feat, 4 * PACK)
    return rows, jnp.asarray(pick, BF16), w_mid, ends, jnp.asarray(place, BF16), jnp.tile(bias, (1, PACK))


def exchange_kernel(sizes, x, out, slots, send, recv):
    count = math.prod(sizes)
    me = (lax.axis_index("shot") * sizes[1] + lax.axis_index("line")) * sizes[2] + lax.axis_index("tm")

    def peer(off):
        at = lax.rem(me + off, count)
        return {
            "shot": at // (sizes[1] * sizes[2]),
            "line": lax.rem(at // sizes[2], sizes[1]),
            "tm": lax.rem(at, sizes[2]),
        }

    barrier = pltpu.get_barrier_semaphore()
    for off in range(1, count):
        pl.semaphore_signal(barrier, inc=1, device_id=peer(off), device_id_type=pl.DeviceIdType.MESH)
    pl.semaphore_wait(barrier, count - 1)
    copies = []
    for off in range(1, count):
        copy = pltpu.make_async_remote_copy(
            src_ref=x,
            dst_ref=slots.at[off],
            send_sem=send.at[off],
            recv_sem=recv.at[off],
            device_id=peer(off),
            device_id_type=pl.DeviceIdType.MESH,
        )
        copy.start()
        copies.append(copy)
    total = x[...]
    for off, copy in enumerate(copies, 1):
        copy.wait()
        total += slots[off]
    out[...] = total


def summed(x, sizes):
    count, v = math.prod(sizes), pl.BlockSpec(memory_space=pltpu.VMEM)
    return pl.pallas_call(
        functools.partial(exchange_kernel, sizes),
        out_shape=jax.ShapeDtypeStruct(x.shape, x.dtype),
        in_specs=[v],
        out_specs=v,
        scratch_shapes=[
            pltpu.VMEM((count, *x.shape), x.dtype),
            pltpu.SemaphoreType.DMA((count,)),
            pltpu.SemaphoreType.DMA((count,)),
        ],
        compiler_params=pltpu.CompilerParams(collective_id=0, has_side_effects=True),
    )(x)


def per_device(guess, mixtures, lags, order, tallies, e1, m1, x1, b1, e2, m2, x2, b2, pace):
    sh, recv, tl = guess.shape
    n_shot, n_line, n_tm = (lax.axis_size(a) for a in AXES)
    whole = RPL % (n_shot * n_line * n_tm) == 0
    where = AXES if whole else AXES[1:]
    parts = math.prod(lax.axis_size(a) for a in where)
    kp, lh = RPL // parts, recv // RPL
    lines, shots, nt = lh * n_line, sh * n_shot, tl * n_tm
    planes, s1 = nt // 2 // C, shots if whole else sh
    r1 = lines * kp
    r2 = r1 if whole else r1 // n_shot
    lanes1, lanes2 = 2 * s1 * r1, 2 * shots * r2
    sources = n_shot if whole else 1
    i32 = functools.partial(jnp.arange, dtype=jnp.int32)

    x = guess.reshape(sh, lh, parts, kp, tl).transpose(2, 0, 1, 3, 4)
    x = lax.all_to_all(x, where, split_axis=0, concat_axis=0)
    fused = whole and sh == 1 and kp == 1 and C % n_tm == 0
    if fused:
        x = x.reshape(parts, lh, tl)
    else:
        x = x.reshape(sources, n_line, n_tm, sh, lh, kp, tl).transpose(0, 3, 1, 4, 5, 2, 6)
        x = x.reshape(s1, r1, C, planes, 2).transpose(3, 2, 4, 0, 1).reshape(planes, C, lanes1)

    at_shot = lax.axis_index("shot")

    def first_k(line):
        block = line * n_tm + lax.axis_index("tm")
        return (at_shot * n_line * n_tm + block if whole else block) * kp

    n_mix = mixtures.shape[0]
    grid = mixtures.reshape(n_mix, lh, RPL, nt)
    sent = jnp.stack([lax.dynamic_slice_in_dim(grid, first_k(d), kp, axis=2) for d in range(n_line)])
    m = lax.all_to_all(sent, "line", split_axis=0, concat_axis=0)
    if fused:
        m = m.reshape(n_line, n_mix, lh, nt)
    else:
        m = m.transpose(1, 0, 2, 3, 4).reshape(n_mix, r1, nt)
        if not whole:
            m = lax.dynamic_slice_in_dim(m, at_shot * r2, r2, axis=1)
        m = m.reshape(n_mix, r2, C, planes, 2).transpose(3, 2, 4, 0, 1).reshape(planes * C, 2 * n_mix * r2)

    np_ = tallies.shape[0]
    here = i32(np_)
    offsets = jnp.sum(jnp.where(here[None, :] < here[:, None], tallies[None, :], 0), axis=1)
    mine = first_k(lax.axis_index("line"))

    def one_hot(r):
        line, k = r // kp, mine + lax.rem(r, kp)
        q = lax.rem(line, lh) * RPL + k
        inside = (offsets[:, None] <= q[None, :]) & (q[None, :] < (offsets + tallies)[:, None])
        block = (line // lh)[None, :] == i32(n_line)[:, None]
        return (block[:, None, :] & inside[None, :, :]).reshape(n_line * np_, r.shape[0]).astype(F32)

    member = jnp.tile(one_hot(i32(r1)), (1, 2 * s1))
    r_own = i32(r2) if whole else at_shot * r2 + i32(r2)
    count = jnp.tile((tallies * (shots * nt)).astype(F32), n_line)
    spread = jnp.tile(one_hot(r_own) / count[:, None], (1, 2 * shots))

    sid = i32(shots)
    place = jnp.sum(jnp.where(order[None, :] == sid[:, None], sid[None, :], 0), axis=1)
    group = place // (shots // n_mix)
    same = (group[:, None] == group[None, :]).astype(BF16)
    chosen = (i32(n_mix)[:, None] == group[None, :]).astype(BF16)
    rest, two = jnp.eye(r2, dtype=BF16), jnp.eye(2, dtype=BF16)
    join = jnp.kron(two, jnp.kron(same, rest))
    take = jnp.kron(two, jnp.kron(chosen, rest))

    n1, n2 = s1 * r1, shots * r2
    a, b = np.arange(n1)[:, None], np.arange(n1)[None, :]
    near1 = np.stack([(a == b + (c - 1) * kp) & (a // r1 == b // r1) for c in range(3)])
    a, b = np.arange(n2)[:, None], np.arange(n2)[None, :]
    near2 = np.stack([a == b + (c - 1) * r2 for c in range(3)])
    wa = prepared(e1, m1, x1, b1, near1)
    wb = prepared(e2, m2, x2, b2, near2)

    rows = planes * C
    tot1, tot2 = pltpu.VMEM((rows, 2 * lanes1), F32), pltpu.VMEM((rows, 2 * lanes2), F32)
    feat = e1.shape[2]
    band = pltpu.VMEM((3 * PACK * feat, PACK * feat), BF16)
    buf = pltpu.VMEM((2, 2 * planes, C, lanes2), F32)
    spass = jax.ShapeDtypeStruct((planes, C, lanes1), BF16)
    part = jax.ShapeDtypeStruct((n_line * np_, 128), F32)
    moved = jax.ShapeDtypeStruct((planes, C, lanes2), BF16)

    def to_stations(y):
        y = y.reshape(rows, 2, sh, n_shot, r2)
        y = lax.all_to_all(y, "shot", split_axis=3, concat_axis=2, tiled=True)
        return y.reshape(planes, C, lanes2)

    def to_shots(y):
        y = y.reshape(rows, 2, shots, 1, r2)
        y = lax.all_to_all(y, "shot", split_axis=2, concat_axis=3, tiled=True)
        return y.reshape(planes, C, lanes1)

    dims = (n_shot, n_line, n_tm)
    cube = pltpu.VMEM((planes, C, lanes1), F32)
    if fused:
        mixed = jax.ShapeDtypeStruct((rows, 2 * n_mix * r2), BF16)
        side = pltpu.VMEM((planes, C, 2 * n_mix * r2), F32)
        sp, energy, m = call(
            functools.partial(entry_kernel, dims),
            (spass, part, mixed),
            (x, m, *wa, member),
            0,
            [tot1, band, cube, side],
        )
    else:
        sp, energy = call(first_kernel, (spass, part), (x, *wa, member), 0, [tot1, band])
    for it in range(ITERS):
        tot = summed(energy, (n_shot, n_line, n_tm)) if whole else lax.psum(energy, AXES)
        if not whole:
            sp = to_stations(sp)
        ins = (lags, pace, sp, tot, spread, *wb, join, m, take)
        if whole and it < ITERS - 1:
            sp, energy = call(
                functools.partial(both_kernel, it, shots), (spass, part), (*ins, *wa, member), 2, [buf, tot2, band]
            )
            continue
        if fused:
            back = jax.ShapeDtypeStruct((parts, lh, tl), BF16)
            x = call(functools.partial(exit_kernel, it, dims), back, ins, 2, [buf, tot2, band, cube])
            continue
        x = call(functools.partial(station_kernel, it, shots), moved, ins, 2, [buf, tot2, band])
        if not whole:
            x = to_shots(x)
            if it < ITERS - 1:
                sp, energy = call(first_kernel, (spass, part), (x, *wa, member), 0, [tot1, band])

    if not fused:
        x = x.reshape(planes, C, 2, s1, r1).transpose(3, 4, 1, 0, 2)
        x = x.reshape(sources, sh, n_line, lh, kp, n_tm, tl).transpose(0, 2, 5, 1, 3, 4, 6)
    x = lax.all_to_all(x.reshape(parts, sh, lh, kp, tl), where, split_axis=0, concat_axis=0)
    return x.transpose(1, 2, 0, 3, 4).reshape(sh, recv, tl)


def solution(mesh):
    spec = P(("group", "shot"), "line", "tm")
    placed = (spec, P("group", "line", None), P("group"), P("group"), P("group")) + (P(),) * 9
    return jax.shard_map(per_device, mesh=mesh, in_specs=placed, out_specs=spec, check_vma=False)
```

```python
import functools
import math

import jax
import jax.numpy as jnp
import numpy as np
from jax import lax
from jax.experimental import pallas as pl
from jax.experimental.pallas import tpu as pltpu
from jax.sharding import PartitionSpec as P

RPL = 16
ITERS = 2
EPSILON = 1e-05
C = 8
PACK = 4
TAPS = (1, 2, 3, 0)
F32, BF16 = jnp.float32, jnp.bfloat16
AXES = ("shot", "line", "tm")


def ahead(x, k):
    edge = pltpu.roll(x[:k], C - 1, 1)
    edge = jnp.where(lax.broadcasted_iota(jnp.int32, edge.shape, 1) == C - 1, 0.0, edge)
    return edge if k == x.shape[0] else jnp.concatenate([x[k:], edge], axis=0)


def behind(x, k):
    edge = pltpu.roll(x[x.shape[0] - k :], 1, 1)
    edge = jnp.where(lax.broadcasted_iota(jnp.int32, edge.shape, 1) == 0, 0.0, edge)
    return edge if k == x.shape[0] else jnp.concatenate([edge, x[: x.shape[0] - k]], axis=0)


def even_lanes(shape):
    return lax.broadcasted_iota(jnp.int32, shape, len(shape) - 1) < shape[-1] // 2


def net(x, w_in, pick, w_mid, w_out, place, bias, total, band):
    planes, _, lanes = x.shape
    rows = planes * C
    side = jnp.where(even_lanes(x.shape), ahead(x, 1), behind(x, 1))
    z = jnp.concatenate([x, side], axis=2).astype(BF16).reshape(rows, 2 * lanes)
    total[...] = jnp.zeros_like(total)
    wide = w_in.shape[1]
    feat = wide // PACK
    for j in range(3):
        tap = w_mid[j].astype(F32)
        for i in range(PACK):
            row = [tap if p == i else jnp.zeros_like(tap) for p in range(PACK)]
            at = (j * PACK + i) * feat
            band[at : at + feat, :] = jnp.concatenate(row, axis=1).astype(BF16)

    def step(q, carry):
        w_here = jnp.dot(pick[q], w_in[...], preferred_element_type=F32).astype(BF16)
        o_here = jnp.dot(w_out[...], place[q], preferred_element_type=F32).astype(BF16)
        h = jnp.dot(z, w_here, preferred_element_type=F32)
        h = jnp.maximum(h + bias[0:1, :], 0.0)
        cube = h.reshape(planes, C, wide)
        first = ahead(cube[:2], 2).reshape(2 * C, wide).astype(BF16)
        last = behind(cube[planes - 2 :], 2).reshape(2 * C, wide).astype(BF16)
        hb = h.astype(BF16)
        early = jnp.concatenate([last, hb[: rows - 2 * C]], axis=0)
        late = jnp.concatenate([hb[2 * C :], first], axis=0)
        g = jnp.dot(jnp.concatenate([early, hb, late], axis=1), band[...], preferred_element_type=F32)
        g = jnp.maximum(g + bias[1:2, :], 0.0).astype(BF16)
        total[...] += jnp.dot(g, o_here, preferred_element_type=F32)
        return carry

    lax.fori_loop(0, pick.shape[0], step, 0, unroll=2)
    y = total[...].reshape(planes, C, 2 * lanes)
    a, b = y[:, :, :lanes], y[:, :, lanes:]
    return a + jnp.where(even_lanes(b.shape), behind(b, 1), ahead(b, 1))


def shot_step(x, weights, member, out_ref, part_ref, total, band):
    y = (x + net(x, *weights, total, band)).astype(BF16)
    out_ref[...] = y
    y = y.astype(F32)
    energy = jnp.sum(jnp.sum(y * y, axis=0), axis=0, keepdims=True)
    sums = jnp.sum(member[...] * energy, axis=1, keepdims=True)
    part_ref[...] = jnp.broadcast_to(sums, part_ref.shape)


def shifted(buf, lag_ref, shots, forward):
    planes, lanes = buf.shape[1] // 2, buf.shape[3]
    shape = (planes, C, lanes)
    even = even_lanes(shape)
    per = lanes // 2 // shots
    lane_shot = lax.rem(lax.broadcasted_iota(jnp.int32, shape, 2), lanes // 2) // per
    out = jnp.zeros(shape, F32)
    for s in range(shots):
        lag = lag_ref[s]
        half, odd = lag // 2, lax.rem(lag, 2)
        at_even = half if forward else planes - half - odd
        at_odd = half + odd if forward else planes - half
        one = jnp.where(even, buf[odd, pl.ds(at_even, planes)], buf[odd, pl.ds(at_odd, planes)])
        out = jnp.where(lane_shot == s, one, out)
    return out


def station_step(shots, sp, tot_ref, spread, weights, lags, join, mix, take, pace, buf, total, band):
    planes, _, lanes = sp.shape
    rows = planes * C
    mean = jnp.sum(tot_ref[:, 0:1] * spread[...], axis=0, keepdims=True)
    rms = jnp.sqrt(mean + EPSILON).reshape(1, 1, lanes)
    normed = (sp / rms).astype(BF16).astype(F32)
    settled = (sp + rms * net(normed, *weights, total, band)).astype(BF16).astype(F32)

    def fill(x, forward):
        far = ahead(x, planes) if forward else behind(x, planes)
        near_at, far_at = (0, planes) if forward else (planes, 0)
        for v, at in ((x, near_at), (far, far_at)):
            buf[0, at : at + planes] = v
            h = lanes // 2
            buf[1, at : at + planes] = jnp.concatenate([v[:, :, h:], v[:, :, :h]], axis=2)

    fill(settled, False)
    fired = shifted(buf, lags, shots, False).astype(BF16).reshape(rows, lanes)
    misfit = jnp.dot(fired, join[...], preferred_element_type=F32)
    misfit -= jnp.dot(mix[...], take[...], preferred_element_type=F32)
    fill(misfit.reshape(planes, C, lanes), True)
    return (settled - pace * shifted(buf, lags, shots, True)).astype(BF16)


def by_phase(width):
    row = lax.broadcasted_iota(jnp.int32, (width, width), 0)
    col = lax.broadcasted_iota(jnp.int32, (width, width), 1)
    half = width // 2
    return jnp.where(col == 2 * lax.rem(row, half) + row // half, 1.0, 0.0).astype(BF16)


def unfold(read, into, sort):
    planes = into.shape[0]
    for c in range(C):
        v = lax.dot_general(sort, read(c), (((1,), (1,)), ((), ())), preferred_element_type=F32)
        into[:, c, :] = jnp.concatenate([v[:planes], v[planes:]], axis=1)


def entry_kernel(
    dims, x, m, wi, wp, wm, wo, wq, bi, member, out, part, mix, total, band, cube, side
):
    shots, blocks, halves = dims
    width = 2 * cube.shape[0]
    sort, each = by_phase(width), C // halves

    def traces(c):
        t, fold, lh = c // each, each // 2, x.shape[1] // 2
        row, at = c % each // fold * lh, slice(c % fold * width, (c % fold + 1) * width)
        rows = [
            x[(s * blocks + b) * halves + t].astype(F32)[row : row + lh, at] for s in range(shots) for b in range(blocks)
        ]
        return jnp.concatenate(rows, axis=0).astype(BF16)

    def records(c):
        at = slice(c * width, (c + 1) * width)
        rows = [m[b, g, :, at].astype(F32) for g in range(m.shape[1]) for b in range(blocks)]
        return jnp.concatenate(rows, axis=0).astype(BF16)

    unfold(records, side, sort)
    mix[...] = side[...].astype(BF16).reshape(mix.shape)
    unfold(traces, cube, sort)
    shot_step(cube[...], (wi, wp, wm, wo, wq, bi), member, out, part, total, band)


def exit_kernel(
    it, dims, lags, pace, sp, tot, spread, wi, wp, wm, wo, wq, bi, join, mix, take, out, buf, total, band, cube
):
    shots, blocks, halves = dims
    width = 2 * cube.shape[0]
    sort, each = by_phase(width), C // halves
    x = station_step(
        shots, sp[...].astype(F32), tot, spread, (wi, wp, wm, wo, wq, bi), lags, join, mix, take, pace[it], buf, total, band
    )
    cube[...] = x.astype(F32)
    n, lh = cube.shape[2] // 2, out.shape[1] // 2
    fold = each // 2
    for c in range(C):
        v = cube[:, c, :]
        v = jnp.concatenate([v[:, :n], v[:, n:]], axis=0).T.astype(BF16)
        v = jnp.dot(v, sort, preferred_element_type=F32)
        t = c // each
        row, at = c % each // fold * lh, slice(c % fold * width, (c % fold + 1) * width)
        for j in range(shots * blocks):
            out[j * halves + t, row : row + lh, at] = v[j * lh : (j + 1) * lh].astype(BF16)


def first_kernel(x, wi, wp, wm, wo, wq, bi, member, out, part, total, band):
    shot_step(x[...].astype(F32), (wi, wp, wm, wo, wq, bi), member, out, part, total, band)


def station_kernel(it, shots, lags, pace, sp, tot, spread, wi, wp, wm, wo, wq, bi, join, mix, take, out, buf, total, band):
    out[...] = station_step(
        shots, sp[...].astype(F32), tot, spread, (wi, wp, wm, wo, wq, bi), lags, join, mix, take, pace[it], buf, total, band
    )


def both_kernel(
    it, shots, lags, pace, sp, tot, spread, wi, wp, wm, wo, wq, bi, join, mix, take, vi, vp, vm, vo, vq, ci, member, out, part, buf, total, band
):
    x = station_step(
        shots, sp[...].astype(F32), tot, spread, (wi, wp, wm, wo, wq, bi), lags, join, mix, take, pace[it], buf, total, band
    )
    shot_step(x.astype(F32), (vi, vp, vm, vo, vq, ci), member, out, part, total, band)


def call(body, outs, ins, smem, scratch):
    v, s = pl.BlockSpec(memory_space=pltpu.VMEM), pl.BlockSpec(memory_space=pltpu.SMEM)
    return pl.pallas_call(
        body,
        out_shape=outs,
        in_specs=[s] * smem + [v] * (len(ins) - smem),
        out_specs=jax.tree.map(lambda _: v, outs),
        scratch_shapes=scratch,
        compiler_params=pltpu.CompilerParams(vmem_limit_bytes=48 * 2**20),
    )(*ins)


def prepared(w_in, w_mid, w_out, bias, near):
    n, feat = near.shape[1], w_in.shape[2]
    tiles = n // PACK
    cols = near.reshape(3, n, tiles, PACK).transpose(2, 1, 0, 3)
    pick = np.einsum("jk,tnci->tjnkci", np.eye(4)[list(TAPS)], cols).reshape(tiles, 4 * n, 12 * PACK)
    place = np.einsum("kj,tin->tjikn", np.eye(4)[list(TAPS)], np.eye(n).reshape(tiles, PACK, n)).reshape(tiles, 4 * PACK, 4 * n)
    w1 = w_in.reshape(12, 1, 1, feat)
    eye = jnp.eye(PACK, dtype=BF16)
    rows = (w1 * eye[None, :, :, None]).reshape(12 * PACK, PACK * feat)
    w2 = w_out.T.reshape(1, feat, 4, 1)
    ends = (w2 * eye[:, None, None, :]).reshape(PACK * feat, 4 * PACK)
    return rows, jnp.asarray(pick, BF16), w_mid, ends, jnp.asarray(place, BF16), jnp.tile(bias, (1, PACK))


def greeted(sizes):
    count = math.prod(sizes)
    me = (lax.axis_index("shot") * sizes[1] + lax.axis_index("line")) * sizes[2] + lax.axis_index("tm")
    peers = []
    for off in range(1, count):
        at = lax.rem(me + off, count)
        coords = {
            "shot": at // (sizes[1] * sizes[2]),
            "line": lax.rem(at // sizes[2], sizes[1]),
            "tm": lax.rem(at, sizes[2]),
        }
        peers.append((off, at, coords))
    barrier = pltpu.get_barrier_semaphore()
    for _, _, coords in peers:
        pl.semaphore_signal(barrier, inc=1, device_id=coords, device_id_type=pl.DeviceIdType.MESH)
    pl.semaphore_wait(barrier, count - 1)
    return me, peers


def swap_kernel(sizes, x, out, slots, send, recv):
    me, peers = greeted(sizes)
    count = math.prod(sizes)
    copies = []
    for off, at, coords in peers:
        copy = pltpu.make_async_remote_copy(
            src_ref=x.at[at],
            dst_ref=slots.at[off],
            send_sem=send.at[off],
            recv_sem=recv.at[off],
            device_id=coords,
            device_id_type=pl.DeviceIdType.MESH,
        )
        copy.start()
        copies.append(copy)
    out[me] = x[me]
    for off, copy in enumerate(copies, 1):
        copy.wait()
        out[lax.rem(me + count - off, count)] = slots[off]


def swapped(x, sizes):
    count, v = math.prod(sizes), pl.BlockSpec(memory_space=pltpu.VMEM)
    return pl.pallas_call(
        functools.partial(swap_kernel, sizes),
        out_shape=jax.ShapeDtypeStruct(x.shape, x.dtype),
        in_specs=[v],
        out_specs=v,
        scratch_shapes=[
            pltpu.VMEM(x.shape, x.dtype),
            pltpu.SemaphoreType.DMA((count,)),
            pltpu.SemaphoreType.DMA((count,)),
        ],
        compiler_params=pltpu.CompilerParams(collective_id=1, has_side_effects=True),
    )(x)


def exchange_kernel(sizes, x, out, slots, send, recv):
    _, peers = greeted(sizes)
    copies = []
    for off, _, coords in peers:
        copy = pltpu.make_async_remote_copy(
            src_ref=x,
            dst_ref=slots.at[off],
            send_sem=send.at[off],
            recv_sem=recv.at[off],
            device_id=coords,
            device_id_type=pl.DeviceIdType.MESH,
        )
        copy.start()
        copies.append(copy)
    total = x[...]
    for off, copy in enumerate(copies, 1):
        copy.wait()
        total += slots[off]
    out[...] = total


def summed(x, sizes):
    count, v = math.prod(sizes), pl.BlockSpec(memory_space=pltpu.VMEM)
    return pl.pallas_call(
        functools.partial(exchange_kernel, sizes),
        out_shape=jax.ShapeDtypeStruct(x.shape, x.dtype),
        in_specs=[v],
        out_specs=v,
        scratch_shapes=[
            pltpu.VMEM((count, *x.shape), x.dtype),
            pltpu.SemaphoreType.DMA((count,)),
            pltpu.SemaphoreType.DMA((count,)),
        ],
        compiler_params=pltpu.CompilerParams(collective_id=0, has_side_effects=True),
    )(x)


def per_device(guess, mixtures, lags, order, tallies, e1, m1, x1, b1, e2, m2, x2, b2, pace):
    sh, recv, tl = guess.shape
    n_shot, n_line, n_tm = (lax.axis_size(a) for a in AXES)
    whole = RPL % (n_shot * n_line * n_tm) == 0
    where = AXES if whole else AXES[1:]
    parts = math.prod(lax.axis_size(a) for a in where)
    kp, lh = RPL // parts, recv // RPL
    lines, shots, nt = lh * n_line, sh * n_shot, tl * n_tm
    planes, s1 = nt // 2 // C, shots if whole else sh
    r1 = lines * kp
    r2 = r1 if whole else r1 // n_shot
    lanes1, lanes2 = 2 * s1 * r1, 2 * shots * r2
    sources = n_shot if whole else 1
    i32 = functools.partial(jnp.arange, dtype=jnp.int32)

    fused = whole and sh == 1 and kp == 1 and C % (2 * n_tm) == 0 and 2 * lh % 16 == 0
    sizes = (n_shot, n_line, n_tm)
    if fused:
        x = guess.reshape(lh, parts, 2, tl // 2).transpose(1, 2, 0, 3).reshape(parts, 2 * lh, tl // 2)
        x = swapped(x, sizes)
    else:
        x = guess.reshape(sh, lh, parts, kp, tl).transpose(2, 0, 1, 3, 4)
        x = lax.all_to_all(x, where, split_axis=0, concat_axis=0)
        x = x.reshape(sources, n_line, n_tm, sh, lh, kp, tl).transpose(0, 3, 1, 4, 5, 2, 6)
        x = x.reshape(s1, r1, C, planes, 2).transpose(3, 2, 4, 0, 1).reshape(planes, C, lanes1)

    at_shot = lax.axis_index("shot")

    def first_k(line):
        block = line * n_tm + lax.axis_index("tm")
        return (at_shot * n_line * n_tm + block if whole else block) * kp

    n_mix = mixtures.shape[0]
    grid = mixtures.reshape(n_mix, lh, RPL, nt)
    sent = jnp.stack([lax.dynamic_slice_in_dim(grid, first_k(d), kp, axis=2) for d in range(n_line)])
    m = lax.all_to_all(sent, "line", split_axis=0, concat_axis=0)
    if fused:
        m = m.reshape(n_line, n_mix, lh, nt)
    else:
        m = m.transpose(1, 0, 2, 3, 4).reshape(n_mix, r1, nt)
        if not whole:
            m = lax.dynamic_slice_in_dim(m, at_shot * r2, r2, axis=1)
        m = m.reshape(n_mix, r2, C, planes, 2).transpose(3, 2, 4, 0, 1).reshape(planes * C, 2 * n_mix * r2)

    np_ = tallies.shape[0]
    here = i32(np_)
    offsets = jnp.sum(jnp.where(here[None, :] < here[:, None], tallies[None, :], 0), axis=1)
    mine = first_k(lax.axis_index("line"))

    def one_hot(r):
        line, k = r // kp, mine + lax.rem(r, kp)
        q = lax.rem(line, lh) * RPL + k
        inside = (offsets[:, None] <= q[None, :]) & (q[None, :] < (offsets + tallies)[:, None])
        block = (line // lh)[None, :] == i32(n_line)[:, None]
        return (block[:, None, :] & inside[None, :, :]).reshape(n_line * np_, r.shape[0]).astype(F32)

    member = jnp.tile(one_hot(i32(r1)), (1, 2 * s1))
    r_own = i32(r2) if whole else at_shot * r2 + i32(r2)
    count = jnp.tile((tallies * (shots * nt)).astype(F32), n_line)
    spread = jnp.tile(one_hot(r_own) / count[:, None], (1, 2 * shots))

    sid = i32(shots)
    place = jnp.sum(jnp.where(order[None, :] == sid[:, None], sid[None, :], 0), axis=1)
    group = place // (shots // n_mix)
    same = (group[:, None] == group[None, :]).astype(BF16)
    chosen = (i32(n_mix)[:, None] == group[None, :]).astype(BF16)
    rest, two = jnp.eye(r2, dtype=BF16), jnp.eye(2, dtype=BF16)
    join = jnp.kron(two, jnp.kron(same, rest))
    take = jnp.kron(two, jnp.kron(chosen, rest))

    n1, n2 = s1 * r1, shots * r2
    a, b = np.arange(n1)[:, None], np.arange(n1)[None, :]
    near1 = np.stack([(a == b + (c - 1) * kp) & (a // r1 == b // r1) for c in range(3)])
    a, b = np.arange(n2)[:, None], np.arange(n2)[None, :]
    near2 = np.stack([a == b + (c - 1) * r2 for c in range(3)])
    wa = prepared(e1, m1, x1, b1, near1)
    wb = prepared(e2, m2, x2, b2, near2)

    rows = planes * C
    tot1, tot2 = pltpu.VMEM((rows, 2 * lanes1), F32), pltpu.VMEM((rows, 2 * lanes2), F32)
    feat = e1.shape[2]
    band = pltpu.VMEM((3 * PACK * feat, PACK * feat), BF16)
    buf = pltpu.VMEM((2, 2 * planes, C, lanes2), F32)
    spass = jax.ShapeDtypeStruct((planes, C, lanes1), BF16)
    part = jax.ShapeDtypeStruct((n_line * np_, 128), F32)
    moved = jax.ShapeDtypeStruct((planes, C, lanes2), BF16)

    def to_stations(y):
        y = y.reshape(rows, 2, sh, n_shot, r2)
        y = lax.all_to_all(y, "shot", split_axis=3, concat_axis=2, tiled=True)
        return y.reshape(planes, C, lanes2)

    def to_shots(y):
        y = y.reshape(rows, 2, shots, 1, r2)
        y = lax.all_to_all(y, "shot", split_axis=2, concat_axis=3, tiled=True)
        return y.reshape(planes, C, lanes1)

    dims = (n_shot, n_line, n_tm)
    cube = pltpu.VMEM((planes, C, lanes1), F32)
    if fused:
        mixed = jax.ShapeDtypeStruct((rows, 2 * n_mix * r2), BF16)
        side = pltpu.VMEM((planes, C, 2 * n_mix * r2), F32)
        sp, energy, m = call(
            functools.partial(entry_kernel, dims),
            (spass, part, mixed),
            (x, m, *wa, member),
            0,
            [tot1, band, cube, side],
        )
    else:
        sp, energy = call(first_kernel, (spass, part), (x, *wa, member), 0, [tot1, band])
    for it in range(ITERS):
        tot = summed(energy, (n_shot, n_line, n_tm)) if whole else lax.psum(energy, AXES)
        if not whole:
            sp = to_stations(sp)
        ins = (lags, pace, sp, tot, spread, *wb, join, m, take)
        if whole and it < ITERS - 1:
            sp, energy = call(
                functools.partial(both_kernel, it, shots), (spass, part), (*ins, *wa, member), 2, [buf, tot2, band]
            )
            continue
        if fused:
            back = jax.ShapeDtypeStruct((parts, 2 * lh, tl // 2), BF16)
            x = call(functools.partial(exit_kernel, it, dims), back, ins, 2, [buf, tot2, band, cube])
            continue
        x = call(functools.partial(station_kernel, it, shots), moved, ins, 2, [buf, tot2, band])
        if not whole:
            x = to_shots(x)
            if it < ITERS - 1:
                sp, energy = call(first_kernel, (spass, part), (x, *wa, member), 0, [tot1, band])

    if fused:
        x = swapped(x, sizes).reshape(parts, 2, lh, tl // 2)
        return x.transpose(2, 0, 1, 3).reshape(sh, recv, tl)
    if not fused:
        x = x.reshape(planes, C, 2, s1, r1).transpose(3, 4, 1, 0, 2)
        x = x.reshape(sources, sh, n_line, lh, kp, n_tm, tl).transpose(0, 2, 5, 1, 3, 4, 6)
    x = lax.all_to_all(x.reshape(parts, sh, lh, kp, tl), where, split_axis=0, concat_axis=0)
    return x.transpose(1, 2, 0, 3, 4).reshape(sh, recv, tl)


def solution(mesh):
    spec = P(("group", "shot"), "line", "tm")
    placed = (spec, P("group", "line", None), P("group"), P("group"), P("group")) + (P(),) * 9
    return jax.shard_map(per_device, mesh=mesh, in_specs=placed, out_specs=spec, check_vma=False)
```

```python
import functools
import math

import jax
import jax.numpy as jnp
import numpy as np
from jax import lax
from jax.experimental import pallas as pl
from jax.experimental.pallas import tpu as pltpu
from jax.sharding import PartitionSpec as P

RPL = 16
ITERS = 2
EPSILON = 1e-05
C = 8
PACK = 4
TAPS = (1, 2, 3, 0)
F32, BF16 = jnp.float32, jnp.bfloat16
AXES = ("shot", "line", "tm")


def ahead(x, k):
    edge = pltpu.roll(x[:k], C - 1, 1)
    edge = jnp.where(lax.broadcasted_iota(jnp.int32, edge.shape, 1) == C - 1, 0.0, edge)
    return edge if k == x.shape[0] else jnp.concatenate([x[k:], edge], axis=0)


def behind(x, k):
    edge = pltpu.roll(x[x.shape[0] - k :], 1, 1)
    edge = jnp.where(lax.broadcasted_iota(jnp.int32, edge.shape, 1) == 0, 0.0, edge)
    return edge if k == x.shape[0] else jnp.concatenate([edge, x[: x.shape[0] - k]], axis=0)


def even_lanes(shape):
    return lax.broadcasted_iota(jnp.int32, shape, len(shape) - 1) < shape[-1] // 2


def net(x, w_in, pick, w_mid, w_out, place, bias, total, band):
    planes, _, lanes = x.shape
    rows = planes * C
    side = jnp.where(even_lanes(x.shape), ahead(x, 1), behind(x, 1))
    z = jnp.concatenate([x, side], axis=2).astype(BF16).reshape(rows, 2 * lanes)
    total[...] = jnp.zeros_like(total)
    wide = w_in.shape[1]
    feat = wide // PACK
    for j in range(3):
        tap = w_mid[j].astype(F32)
        for i in range(PACK):
            row = [tap if p == i else jnp.zeros_like(tap) for p in range(PACK)]
            at = (j * PACK + i) * feat
            band[at : at + feat, :] = jnp.concatenate(row, axis=1).astype(BF16)

    def step(q, carry):
        w_here = jnp.dot(pick[q], w_in[...], preferred_element_type=F32).astype(BF16)
        o_here = jnp.dot(w_out[...], place[q], preferred_element_type=F32).astype(BF16)
        h = jnp.dot(z, w_here, preferred_element_type=F32)
        h = jnp.maximum(h + bias[0:1, :], 0.0)
        cube = h.reshape(planes, C, wide)
        first = ahead(cube[:2], 2).reshape(2 * C, wide).astype(BF16)
        last = behind(cube[planes - 2 :], 2).reshape(2 * C, wide).astype(BF16)
        hb = h.astype(BF16)
        early = jnp.concatenate([last, hb[: rows - 2 * C]], axis=0)
        late = jnp.concatenate([hb[2 * C :], first], axis=0)
        g = jnp.dot(jnp.concatenate([early, hb, late], axis=1), band[...], preferred_element_type=F32)
        g = jnp.maximum(g + bias[1:2, :], 0.0).astype(BF16)
        total[...] += jnp.dot(g, o_here, preferred_element_type=F32)
        return carry

    lax.fori_loop(0, pick.shape[0], step, 0, unroll=2)
    y = total[...].reshape(planes, C, 2 * lanes)
    a, b = y[:, :, :lanes], y[:, :, lanes:]
    return a + jnp.where(even_lanes(b.shape), behind(b, 1), ahead(b, 1))


def shot_step(x, weights, member, out_ref, part_ref, total, band):
    y = (x + net(x, *weights, total, band)).astype(BF16)
    out_ref[...] = y
    y = y.astype(F32)
    energy = jnp.sum(jnp.sum(y * y, axis=0), axis=0, keepdims=True)
    sums = jnp.sum(member[...] * energy, axis=1, keepdims=True)
    part_ref[...] = jnp.broadcast_to(sums, part_ref.shape)


def shifted(buf, lag_ref, shots, forward):
    planes, lanes = buf.shape[1] // 2, buf.shape[3]
    shape = (planes, C, lanes)
    even = even_lanes(shape)
    per = lanes // 2 // shots
    lane_shot = lax.rem(lax.broadcasted_iota(jnp.int32, shape, 2), lanes // 2) // per
    out = jnp.zeros(shape, F32)
    for s in range(shots):
        lag = lag_ref[s]
        half, odd = lag // 2, lax.rem(lag, 2)
        at_even = half if forward else planes - half - odd
        at_odd = half + odd if forward else planes - half
        one = jnp.where(even, buf[odd, pl.ds(at_even, planes)], buf[odd, pl.ds(at_odd, planes)])
        out = jnp.where(lane_shot == s, one, out)
    return out


def station_step(shots, sp, tot_ref, spread, weights, lags, join, mix, take, pace, buf, total, band):
    planes, _, lanes = sp.shape
    rows = planes * C
    mean = jnp.sum(tot_ref[:, 0:1] * spread[...], axis=0, keepdims=True)
    rms = jnp.sqrt(mean + EPSILON).reshape(1, 1, lanes)
    normed = (sp / rms).astype(BF16).astype(F32)
    settled = (sp + rms * net(normed, *weights, total, band)).astype(BF16).astype(F32)

    def fill(x, forward):
        far = ahead(x, planes) if forward else behind(x, planes)
        near_at, far_at = (0, planes) if forward else (planes, 0)
        for v, at in ((x, near_at), (far, far_at)):
            buf[0, at : at + planes] = v
            h = lanes // 2
            buf[1, at : at + planes] = jnp.concatenate([v[:, :, h:], v[:, :, :h]], axis=2)

    fill(settled, False)
    fired = shifted(buf, lags, shots, False).astype(BF16).reshape(rows, lanes)
    misfit = jnp.dot(fired, join[...], preferred_element_type=F32)
    misfit -= jnp.dot(mix[...], take[...], preferred_element_type=F32)
    fill(misfit.reshape(planes, C, lanes), True)
    return (settled - pace * shifted(buf, lags, shots, True)).astype(BF16)


def by_phase(width):
    row = lax.broadcasted_iota(jnp.int32, (width, width), 0)
    col = lax.broadcasted_iota(jnp.int32, (width, width), 1)
    half = width // 2
    return jnp.where(col == 2 * lax.rem(row, half) + row // half, 1.0, 0.0).astype(BF16)


def unfold(read, into, sort):
    planes = into.shape[0]
    for c in range(C):
        v = lax.dot_general(sort, read(c), (((1,), (1,)), ((), ())), preferred_element_type=F32)
        into[:, c, :] = jnp.concatenate([v[:planes], v[planes:]], axis=1)


def entry_kernel(
    dims, x, wi, wp, wm, wo, wq, bi, member, out, part, mix, total, band, cube, side
):
    shots, blocks, halves = dims
    width = 2 * cube.shape[0]
    sort, each = by_phase(width), C // halves

    def traces(c):
        at, t = slice(c % each * width, (c % each + 1) * width), c // each
        rows = [x[(s * blocks + b) * halves + t, :, at].astype(F32) for s in range(shots) for b in range(blocks)]
        return jnp.concatenate(rows, axis=0).astype(BF16)

    tl = each * width

    def records(c):
        s, t = c // halves, c % halves
        rows = [
            x[(s * blocks + b) * halves + t, :, tl + g * width : tl + (g + 1) * width].astype(F32)
            for g in range((x.shape[2] - tl) // width)
            for b in range(blocks)
        ]
        return jnp.concatenate(rows, axis=0).astype(BF16)

    unfold(records, side, sort)
    mix[...] = side[...].astype(BF16).reshape(mix.shape)
    unfold(traces, cube, sort)
    shot_step(cube[...], (wi, wp, wm, wo, wq, bi), member, out, part, total, band)


def exit_kernel(
    it, dims, lags, pace, sp, tot, spread, wi, wp, wm, wo, wq, bi, join, mix, take, out, buf, total, band, cube
):
    shots, blocks, halves = dims
    width = 2 * cube.shape[0]
    sort, each = by_phase(width), C // halves
    x = station_step(
        shots, sp[...].astype(F32), tot, spread, (wi, wp, wm, wo, wq, bi), lags, join, mix, take, pace[it], buf, total, band
    )
    cube[...] = x.astype(F32)
    n, lh = cube.shape[2] // 2, out.shape[1]
    for c in range(C):
        v = cube[:, c, :]
        v = jnp.concatenate([v[:, :n], v[:, n:]], axis=0).T.astype(BF16)
        v = jnp.dot(v, sort, preferred_element_type=F32)
        at, t = slice(c % each * width, (c % each + 1) * width), c // each
        for j in range(shots * blocks):
            out[j * halves + t, :, at] = v[j * lh : (j + 1) * lh].astype(BF16)


def first_kernel(x, wi, wp, wm, wo, wq, bi, member, out, part, total, band):
    shot_step(x[...].astype(F32), (wi, wp, wm, wo, wq, bi), member, out, part, total, band)


def station_kernel(it, shots, lags, pace, sp, tot, spread, wi, wp, wm, wo, wq, bi, join, mix, take, out, buf, total, band):
    out[...] = station_step(
        shots, sp[...].astype(F32), tot, spread, (wi, wp, wm, wo, wq, bi), lags, join, mix, take, pace[it], buf, total, band
    )


def both_kernel(
    it, shots, lags, pace, sp, tot, spread, wi, wp, wm, wo, wq, bi, join, mix, take, vi, vp, vm, vo, vq, ci, member, out, part, buf, total, band
):
    x = station_step(
        shots, sp[...].astype(F32), tot, spread, (wi, wp, wm, wo, wq, bi), lags, join, mix, take, pace[it], buf, total, band
    )
    shot_step(x.astype(F32), (vi, vp, vm, vo, vq, ci), member, out, part, total, band)


def call(body, outs, ins, smem, scratch):
    v, s = pl.BlockSpec(memory_space=pltpu.VMEM), pl.BlockSpec(memory_space=pltpu.SMEM)
    return pl.pallas_call(
        body,
        out_shape=outs,
        in_specs=[s] * smem + [v] * (len(ins) - smem),
        out_specs=jax.tree.map(lambda _: v, outs),
        scratch_shapes=scratch,
        compiler_params=pltpu.CompilerParams(vmem_limit_bytes=48 * 2**20),
    )(*ins)


def prepared(w_in, w_mid, w_out, bias, near):
    n, feat = near.shape[1], w_in.shape[2]
    tiles = n // PACK
    cols = near.reshape(3, n, tiles, PACK).transpose(2, 1, 0, 3)
    pick = np.einsum("jk,tnci->tjnkci", np.eye(4)[list(TAPS)], cols).reshape(tiles, 4 * n, 12 * PACK)
    place = np.einsum("kj,tin->tjikn", np.eye(4)[list(TAPS)], np.eye(n).reshape(tiles, PACK, n)).reshape(tiles, 4 * PACK, 4 * n)
    w1 = w_in.reshape(12, 1, 1, feat)
    eye = jnp.eye(PACK, dtype=BF16)
    rows = (w1 * eye[None, :, :, None]).reshape(12 * PACK, PACK * feat)
    w2 = w_out.T.reshape(1, feat, 4, 1)
    ends = (w2 * eye[:, None, None, :]).reshape(PACK * feat, 4 * PACK)
    return rows, jnp.asarray(pick, BF16), w_mid, ends, jnp.asarray(place, BF16), jnp.tile(bias, (1, PACK))


def exchange_kernel(sizes, x, out, slots, send, recv):
    count = math.prod(sizes)
    me = (lax.axis_index("shot") * sizes[1] + lax.axis_index("line")) * sizes[2] + lax.axis_index("tm")

    def peer(off):
        at = lax.rem(me + off, count)
        return {
            "shot": at // (sizes[1] * sizes[2]),
            "line": lax.rem(at // sizes[2], sizes[1]),
            "tm": lax.rem(at, sizes[2]),
        }

    barrier = pltpu.get_barrier_semaphore()
    for off in range(1, count):
        pl.semaphore_signal(barrier, inc=1, device_id=peer(off), device_id_type=pl.DeviceIdType.MESH)
    pl.semaphore_wait(barrier, count - 1)
    copies = []
    for off in range(1, count):
        copy = pltpu.make_async_remote_copy(
            src_ref=x,
            dst_ref=slots.at[off],
            send_sem=send.at[off],
            recv_sem=recv.at[off],
            device_id=peer(off),
            device_id_type=pl.DeviceIdType.MESH,
        )
        copy.start()
        copies.append(copy)
    total = x[...]
    for off, copy in enumerate(copies, 1):
        copy.wait()
        total += slots[off]
    out[...] = total


def summed(x, sizes):
    count, v = math.prod(sizes), pl.BlockSpec(memory_space=pltpu.VMEM)
    return pl.pallas_call(
        functools.partial(exchange_kernel, sizes),
        out_shape=jax.ShapeDtypeStruct(x.shape, x.dtype),
        in_specs=[v],
        out_specs=v,
        scratch_shapes=[
            pltpu.VMEM((count, *x.shape), x.dtype),
            pltpu.SemaphoreType.DMA((count,)),
            pltpu.SemaphoreType.DMA((count,)),
        ],
        compiler_params=pltpu.CompilerParams(collective_id=0, has_side_effects=True),
    )(x)


def per_device(guess, mixtures, lags, order, tallies, e1, m1, x1, b1, e2, m2, x2, b2, pace):
    sh, recv, tl = guess.shape
    n_shot, n_line, n_tm = (lax.axis_size(a) for a in AXES)
    whole = RPL % (n_shot * n_line * n_tm) == 0
    where = AXES if whole else AXES[1:]
    parts = math.prod(lax.axis_size(a) for a in where)
    kp, lh = RPL // parts, recv // RPL
    lines, shots, nt = lh * n_line, sh * n_shot, tl * n_tm
    planes, s1 = nt // 2 // C, shots if whole else sh
    r1 = lines * kp
    r2 = r1 if whole else r1 // n_shot
    lanes1, lanes2 = 2 * s1 * r1, 2 * shots * r2
    sources = n_shot if whole else 1
    i32 = functools.partial(jnp.arange, dtype=jnp.int32)

    at_shot = lax.axis_index("shot")
    n_mix, run = mixtures.shape[0], nt // C
    fused = whole and sh == 1 and kp == 1 and C % n_tm == 0 and n_shot * n_tm == C
    x = guess.reshape(sh, lh, parts, kp, tl).transpose(2, 0, 1, 3, 4)
    if fused:
        share = (at_shot * n_tm + lax.axis_index("tm")) * run
        mine = lax.dynamic_slice_in_dim(mixtures, share, run, axis=2).reshape(n_mix, lh, parts, run)
        mine = mine.transpose(2, 1, 0, 3).reshape(parts, lh, n_mix * run)
        x = jnp.concatenate([x.reshape(parts, lh, tl), mine], axis=2)
    x = lax.all_to_all(x, where, split_axis=0, concat_axis=0, tiled=False)
    if not fused:
        x = x.reshape(sources, n_line, n_tm, sh, lh, kp, tl).transpose(0, 3, 1, 4, 5, 2, 6)
        x = x.reshape(s1, r1, C, planes, 2).transpose(3, 2, 4, 0, 1).reshape(planes, C, lanes1)


    def first_k(line):
        block = line * n_tm + lax.axis_index("tm")
        return (at_shot * n_line * n_tm + block if whole else block) * kp

    if not fused:
        grid = mixtures.reshape(n_mix, lh, RPL, nt)
        sent = jnp.stack([lax.dynamic_slice_in_dim(grid, first_k(d), kp, axis=2) for d in range(n_line)])
        m = lax.all_to_all(sent, "line", split_axis=0, concat_axis=0)
        m = m.transpose(1, 0, 2, 3, 4).reshape(n_mix, r1, nt)
        if not whole:
            m = lax.dynamic_slice_in_dim(m, at_shot * r2, r2, axis=1)
        m = m.reshape(n_mix, r2, C, planes, 2).transpose(3, 2, 4, 0, 1).reshape(planes * C, 2 * n_mix * r2)

    np_ = tallies.shape[0]
    here = i32(np_)
    offsets = jnp.sum(jnp.where(here[None, :] < here[:, None], tallies[None, :], 0), axis=1)
    mine = first_k(lax.axis_index("line"))

    def one_hot(r):
        line, k = r // kp, mine + lax.rem(r, kp)
        q = lax.rem(line, lh) * RPL + k
        inside = (offsets[:, None] <= q[None, :]) & (q[None, :] < (offsets + tallies)[:, None])
        block = (line // lh)[None, :] == i32(n_line)[:, None]
        return (block[:, None, :] & inside[None, :, :]).reshape(n_line * np_, r.shape[0]).astype(F32)

    member = jnp.tile(one_hot(i32(r1)), (1, 2 * s1))
    r_own = i32(r2) if whole else at_shot * r2 + i32(r2)
    count = jnp.tile((tallies * (shots * nt)).astype(F32), n_line)
    spread = jnp.tile(one_hot(r_own) / count[:, None], (1, 2 * shots))

    sid = i32(shots)
    place = jnp.sum(jnp.where(order[None, :] == sid[:, None], sid[None, :], 0), axis=1)
    group = place // (shots // n_mix)
    same = (group[:, None] == group[None, :]).astype(BF16)
    chosen = (i32(n_mix)[:, None] == group[None, :]).astype(BF16)
    rest, two = jnp.eye(r2, dtype=BF16), jnp.eye(2, dtype=BF16)
    join = jnp.kron(two, jnp.kron(same, rest))
    take = jnp.kron(two, jnp.kron(chosen, rest))

    n1, n2 = s1 * r1, shots * r2
    a, b = np.arange(n1)[:, None], np.arange(n1)[None, :]
    near1 = np.stack([(a == b + (c - 1) * kp) & (a // r1 == b // r1) for c in range(3)])
    a, b = np.arange(n2)[:, None], np.arange(n2)[None, :]
    near2 = np.stack([a == b + (c - 1) * r2 for c in range(3)])
    wa = prepared(e1, m1, x1, b1, near1)
    wb = prepared(e2, m2, x2, b2, near2)

    rows = planes * C
    tot1, tot2 = pltpu.VMEM((rows, 2 * lanes1), F32), pltpu.VMEM((rows, 2 * lanes2), F32)
    feat = e1.shape[2]
    band = pltpu.VMEM((3 * PACK * feat, PACK * feat), BF16)
    buf = pltpu.VMEM((2, 2 * planes, C, lanes2), F32)
    spass = jax.ShapeDtypeStruct((planes, C, lanes1), BF16)
    part = jax.ShapeDtypeStruct((n_line * np_, 128), F32)
    moved = jax.ShapeDtypeStruct((planes, C, lanes2), BF16)

    def to_stations(y):
        y = y.reshape(rows, 2, sh, n_shot, r2)
        y = lax.all_to_all(y, "shot", split_axis=3, concat_axis=2, tiled=True)
        return y.reshape(planes, C, lanes2)

    def to_shots(y):
        y = y.reshape(rows, 2, shots, 1, r2)
        y = lax.all_to_all(y, "shot", split_axis=2, concat_axis=3, tiled=True)
        return y.reshape(planes, C, lanes1)

    dims = (n_shot, n_line, n_tm)
    cube = pltpu.VMEM((planes, C, lanes1), F32)
    if fused:
        mixed = jax.ShapeDtypeStruct((rows, 2 * n_mix * r2), BF16)
        side = pltpu.VMEM((planes, C, 2 * n_mix * r2), F32)
        sp, energy, m = call(
            functools.partial(entry_kernel, dims),
            (spass, part, mixed),
            (x, *wa, member),
            0,
            [tot1, band, cube, side],
        )
    else:
        sp, energy = call(first_kernel, (spass, part), (x, *wa, member), 0, [tot1, band])
    for it in range(ITERS):
        tot = summed(energy, (n_shot, n_line, n_tm)) if whole else lax.psum(energy, AXES)
        if not whole:
            sp = to_stations(sp)
        ins = (lags, pace, sp, tot, spread, *wb, join, m, take)
        if whole and it < ITERS - 1:
            sp, energy = call(
                functools.partial(both_kernel, it, shots), (spass, part), (*ins, *wa, member), 2, [buf, tot2, band]
            )
            continue
        if fused:
            back = jax.ShapeDtypeStruct((parts, lh, tl), BF16)
            x = call(functools.partial(exit_kernel, it, dims), back, ins, 2, [buf, tot2, band, cube])
            continue
        x = call(functools.partial(station_kernel, it, shots), moved, ins, 2, [buf, tot2, band])
        if not whole:
            x = to_shots(x)
            if it < ITERS - 1:
                sp, energy = call(first_kernel, (spass, part), (x, *wa, member), 0, [tot1, band])

    if not fused:
        x = x.reshape(planes, C, 2, s1, r1).transpose(3, 4, 1, 0, 2)
        x = x.reshape(sources, sh, n_line, lh, kp, n_tm, tl).transpose(0, 2, 5, 1, 3, 4, 6)
    x = lax.all_to_all(x.reshape(parts, sh, lh, kp, tl), where, split_axis=0, concat_axis=0)
    return x.transpose(1, 2, 0, 3, 4).reshape(sh, recv, tl)


def solution(mesh):
    spec = P(("group", "shot"), "line", "tm")
    placed = (spec, P("group", "line", None), P("group"), P("group"), P("group")) + (P(),) * 9
    return jax.shard_map(per_device, mesh=mesh, in_specs=placed, out_specs=spec, check_vma=False)
```
